128 devices in a mesh: row: 16 (over y, x), col: 8 (over z, core).
Axes of the slice: x: 4, y: 4, z: 4, core: 2. Of those that a mesh axis runs over, the one named last changes fastest.
Arguments:
- inputs: bfloat16 [512, 16384], P('col', 'row'), may hold values from -6 to 6
- gate_weight: bfloat16 [16384, 26624], P('row', 'col'), may hold values from -0.0625 to 0.0625
- up_weight: bfloat16 [16384, 26624], P('row', 'col'), may hold values from -0.0625 to 0.0625
- gate_pattern: int32 [128, 208], P('row', 'col'), may hold values 0 or 1
- up_pattern: int32 [128, 208], P('row', 'col'), may hold values 0 or 1
- cotangent: bfloat16 [512, 26624], P('row', 'col'), may hold values from -6 to 6
Outputs:
- hidden: bfloat16 [512, 26624], P('row', 'col')
- input_grad: bfloat16 [512, 16384], P('col', 'row')
The draws below stay inside these ranges and needn't reach their ends.
All inputs are finite; a program needn't handle non-finite values. No bound on the sum of `gate_pattern` or of `up_pattern` on one device may be relied on, other than what follows from the above.
Results may differ from the reference program's by a relative error of at most 0.039.
Values may be sent and summed in bfloat16 or wider, within the bound.
A program may use at most 128 MiB of HBM per device.

```python
import jax
import jax.numpy as jnp
from jax import lax

D = 16384
FF = 26624
BLOCK = 128
TOKENS = 512
N_ROW = 16


def plant(drawn, key, low, top_value):
    dims = drawn.shape
    spot = [jax.random.randint(jax.random.fold_in(key, axis), (), 0, dims[axis]) for axis in range(len(dims))]
    drawn = drawn.at[tuple(spot)].set(low)
    longest = dims.index(max(dims))
    spot[longest] = (spot[longest] + 1) % dims[longest]
    return drawn.at[tuple(spot)].set(top_value)


def shard_levels(rng, extent, cuts, low, largest):
    gain = 1.0
    for dim, shards_of in cuts:
        steps = jax.random.uniform(jax.random.fold_in(jax.random.fold_in(rng, 6), dim), (shards_of,), jnp.float32, low / len(cuts), largest / len(cuts))
        gain = gain * jnp.repeat(jnp.exp(steps), extent[dim] // shards_of).reshape((-1,) + (1,) * (len(extent) - 1 - dim))
    return gain


def scatter_about(key, dims, scale, bound, pieces=(), held_as=jnp.bfloat16):
    gain = shard_levels(key, dims, pieces, -0.22, 0.18) if pieces else 1.0
    entries = jax.random.normal(key, dims, jnp.float32) * scale * gain
    return jnp.minimum(jnp.maximum(entries, -bound), bound).astype(held_as)


def setup_inputs(seed: int = 0) -> dict:
    arg_keys = jax.random.split(jax.random.key(seed), 7)
    inputs = scatter_about(arg_keys[0], (TOKENS, D), 1.0, 6.0, ((0, 8), (1, 16)))
    gate_weight = scatter_about(arg_keys[1], (D, FF), (D // 2) ** -0.5, 0.0625, ((0, 16), (1, 8)))
    up_weight = scatter_about(arg_keys[2], (D, FF), (D // 2) ** -0.5, 0.0625, ((0, 16), (1, 8)))
    gate_pattern = plant((jax.random.randint(arg_keys[3], (D // BLOCK, FF // BLOCK), 0, 2) < 1).astype(jnp.int32), jax.random.fold_in(arg_keys[3], 1), 0, 1)
    up_pattern = plant((jax.random.randint(arg_keys[4], (D // BLOCK, FF // BLOCK), 0, 2) < 1).astype(jnp.int32), jax.random.fold_in(arg_keys[4], 1), 0, 1)
    cotangent = scatter_about(arg_keys[5], (TOKENS, FF), 1.0, 6.0, ((0, 16), (1, 8)))
    return {"inputs": inputs, "gate_weight": gate_weight, "up_weight": up_weight, "gate_pattern": gate_pattern, "up_pattern": up_pattern, "cotangent": cotangent}


def expand(weight, pattern):
    height, breadth = weight.shape
    flags = pattern.astype(weight.dtype)
    tiles = weight.reshape(height // BLOCK, BLOCK, breadth // BLOCK, BLOCK) * flags[:, None, :, None]
    return tiles.reshape(height, breadth)


def reference(inputs, gate_weight, up_weight, gate_pattern, up_pattern, cotangent):
    width = D // N_ROW
    tiles = width // BLOCK

    def block_weights(block_index):
        start = (block_index * width).astype(jnp.int32)
        tile_start = (block_index * tiles).astype(jnp.int32)
        gate_block = expand(lax.dynamic_slice_in_dim(gate_weight, start, width, 0), lax.dynamic_slice_in_dim(gate_pattern, tile_start, tiles, 0))
        up_block = expand(lax.dynamic_slice_in_dim(up_weight, start, width, 0), lax.dynamic_slice_in_dim(up_pattern, tile_start, tiles, 0))
        return start, gate_block, up_block

    def forward(block_index, carry):
        gate_sum, up_sum = carry
        start, gate_block, up_block = block_weights(block_index)
        columns = lax.dynamic_slice_in_dim(inputs, start, width, 1)
        part_gate = jnp.dot(columns, gate_block, preferred_element_type=jnp.float32).astype(jnp.bfloat16)
        part_up = jnp.dot(columns, up_block, preferred_element_type=jnp.float32).astype(jnp.bfloat16)
        part_gate, part_up = lax.optimization_barrier((part_gate, part_up))
        return gate_sum + part_gate.astype(jnp.float32), up_sum + part_up.astype(jnp.float32)

    empty = jnp.zeros((TOKENS, FF), jnp.float32)
    gate_sum, up_sum = lax.fori_loop(0, N_ROW, forward, (empty, empty))
    sigmoid_gate = jax.nn.sigmoid(gate_sum)
    activated = gate_sum * sigmoid_gate
    hidden = (activated * up_sum).astype(jnp.bfloat16)
    cotangent_f = cotangent.astype(jnp.float32)
    gate_grad = (cotangent_f * up_sum * sigmoid_gate * (1.0 + gate_sum * (1.0 - sigmoid_gate))).astype(jnp.bfloat16)
    up_grad = (cotangent_f * activated).astype(jnp.bfloat16)
    contract = (((1,), (1,)), ((), ()))

    def backward(block_index, result):
        start, gate_block, up_block = block_weights(block_index)
        piece = lax.dot_general(gate_grad, gate_block, contract, preferred_element_type=jnp.float32)
        piece = piece + lax.dot_general(up_grad, up_block, contract, preferred_element_type=jnp.float32)
        return lax.dynamic_update_slice_in_dim(result, piece, start, 1)

    input_grad = lax.fori_loop(0, N_ROW, backward, jnp.zeros((TOKENS, D), jnp.float32))
    return hidden, input_grad.astype(jnp.bfloat16)
```

```python
import functools

import jax
import jax.numpy as jnp
from jax import lax
from jax.experimental import pallas as pl
from jax.experimental.pallas import tpu as pltpu
from jax.sharding import PartitionSpec as P

BLOCK = 128
SIDE = 4
CHUNK = 256
PIECES = 4
LAGS = (0, 1, 2, 3, 4, 5, 6, 7, 8)
F32 = jnp.float32
BF16 = jnp.bfloat16


def kernel(
    chunks, inputs, gate_w, up_w, gate_pat, up_pat, cot, hidden_out, grad_out,
    toks, weights, part, half1, full1, sum1, half2, full2, grads, acc, zsend, zsib, zhalf, zfull,
    cot_v, hid_v, out_v, send, recv, zs, zr, ws, cs, hs, os,
):
    ch = CHUNK
    hc = ch // 2
    row, col = lax.axis_index("row"), lax.axis_index("col")
    y, x = row // SIDE, row % SIDE
    z, core = col // 2, col % 2
    ym, yp, y2 = (y + 3) % SIDE, (y + 1) % SIDE, (y + 2) % SIDE
    xm, xp, x2 = (x + 3) % SIDE, (x + 1) % SIDE, (x + 2) % SIDE
    zm, zp, z2 = (z + 3) % SIDE, (z + 1) % SIDE, (z + 2) % SIDE
    other = 1 - core

    def at(yy, xx):
        return (yy * SIDE + xx, col)

    def atz(zz, cc):
        return (row, zz * 2 + cc)

    left_x, right_x, left_y, right_y = at(y, xm), at(y, xp), at(ym, x), at(yp, x)
    left_z, right_z, sibling = atz(zm, core), atz(zp, core), atz(z, other)

    def remote(src, dst, s, r, dev):
        return pltpu.make_async_remote_copy(
            src_ref=src, dst_ref=dst, send_sem=s, recv_sem=r,
            device_id=dev, device_id_type=pl.DeviceIdType.MESH,
        )

    def weight_copies(c):
        cols = pl.ds(pl.multiple_of(c * ch, ch), ch)
        return (
            pltpu.make_async_copy(gate_w.at[:, cols], weights.at[c, :, pl.ds(0, ch)], ws.at[c, 0]),
            pltpu.make_async_copy(up_w.at[:, cols], weights.at[c, :, pl.ds(ch, ch)], ws.at[c, 1]),
        )

    def cot_copy(c):
        return pltpu.make_async_copy(cot.at[:, pl.ds(pl.multiple_of(c * ch, ch), ch)], cot_v.at[c], cs.at[c])

    def hid_copy(c):
        return pltpu.make_async_copy(hid_v.at[c], hidden_out.at[:, pl.ds(pl.multiple_of(c * ch, ch), ch)], hs.at[c])

    own_copy = pltpu.make_async_copy(inputs, toks.at[col], zs.at[8])
    own_copy.start()

    @pl.loop(0, chunks)
    def _(c):
        for copy in weight_copies(c):
            copy.start()

    @pl.loop(0, chunks)
    def _(c):
        cot_copy(c).start()

    barrier = pltpu.get_barrier_semaphore()
    for dev in (left_x, right_x, left_y, right_y, left_z, right_z, sibling):
        pl.semaphore_signal(barrier, inc=1, device_id=dev, device_id_type=pl.DeviceIdType.MESH)
    pl.semaphore_wait(barrier, 7)

    mine, from_m, from_p, from_2 = z * 2 + core, zm * 2 + core, zp * 2 + core, z2 * 2 + core
    lo, hi = pl.ds(0, 32), pl.ds(32, 32)

    def spread(src, dst, k, dev):
        return remote(src, dst, zs.at[k], zr.at[k], dev)

    g_left = spread(inputs, toks.at[mine], 0, left_z)
    g_right = spread(inputs, toks.at[mine], 1, right_z)
    g_sib = spread(inputs, toks.at[mine], 2, sibling)
    g_left.start()
    g_right.start()
    g_sib.start()

    def mask(c):
        for copy in weight_copies(c):
            copy.wait()
        for which, pat in enumerate((gate_pat, up_pat)):
            for i in range(weights.shape[1] // BLOCK):
                for j in range(ch // BLOCK):
                    flag = pat[i, c * (ch // BLOCK) + j].astype(F32)
                    rows, cols = pl.ds(i * BLOCK, BLOCK), pl.ds(which * ch + j * BLOCK, BLOCK)
                    weights[c, rows, cols] = (weights[c, rows, cols].astype(F32) * flag).astype(BF16)

    acc[...] = jnp.zeros(acc.shape, F32)
    mask(0)
    g_left.wait_recv()
    f_left = spread(toks.at[from_p, hi], toks.at[from_p, hi], 3, left_z)
    f_left.start()
    s_p = spread(toks.at[from_p], toks.at[from_p], 5, sibling)
    s_p.start()
    g_right.wait_recv()
    f_right = spread(toks.at[from_m, lo], toks.at[from_m, lo], 4, right_z)
    f_right.start()
    s_m = spread(toks.at[from_m], toks.at[from_m], 6, sibling)
    s_m.start()
    f_left.wait_recv()
    f_right.wait_recv()
    s_2 = spread(toks.at[from_2], toks.at[from_2], 7, sibling)
    s_2.start()
    own_copy.wait()
    for copy in (g_sib, s_p, s_m, s_2):
        copy.wait_recv()

    def copies(c, k):
        a, b = pl.ds(0, ch), pl.ds(ch, ch)
        al, ar, bl, br = pl.ds(0, hc), pl.ds(hc, hc), pl.ds(ch, hc), pl.ds(ch + hc, hc)
        first, second, every = pl.ds(0, 2), pl.ds(2, 2), pl.ds(0, 4)
        rows = pl.ds(0, 32)
        xdev, ydev = (left_x, right_x), (left_y, right_y)
        if k == 0:
            srcs = (part.at[c, 0, first, x2], part.at[c, 0, second, x2], part.at[c, 1, y2, first], part.at[c, 1, y2, second])
            dsts = tuple(half1.at[c, i // 2, i % 2] for i in range(4))
            devs = xdev + ydev
        elif k == 1:
            srcs = (part.at[c, 0, every, xm], part.at[c, 0, every, xp], part.at[c, 1, ym], part.at[c, 1, yp])
            dsts = tuple(full1.at[c, i // 2, i % 2] for i in range(4))
            devs = xdev + ydev
        elif k == 2:
            srcs = (
                sum1.at[c, 0, y2, rows, al], sum1.at[c, 0, y2, rows, ar],
                sum1.at[c, 1, x2, rows, al], sum1.at[c, 1, x2, rows, ar],
            )
            dsts = tuple(half2.at[c, i // 2, i % 2] for i in range(4))
            devs = ydev + xdev
        elif k == 3:
            srcs = (sum1.at[c, 0, ym], sum1.at[c, 0, yp], sum1.at[c, 1, xm], sum1.at[c, 1, xp])
            dsts = tuple(full2.at[c, i // 2, i % 2] for i in range(4))
            devs = ydev + xdev
        elif k == 4:
            ga, gb = grads.at[c, y, x, rows, a], grads.at[c, y, x, rows, b]
            srcs = dsts = (ga, ga, gb, gb)
            devs = ydev + xdev
        elif k == 5:
            srcs = dsts = (
                grads.at[c, yp, x, rows, ar], grads.at[c, ym, x, rows, al],
                grads.at[c, y, xp, rows, br], grads.at[c, y, xm, rows, bl],
            )
            devs = ydev + xdev
        elif k == 6:
            ga, gb = grads.at[c, every, x, rows, a], grads.at[c, y, every, rows, b]
            srcs = dsts = (ga, ga, gb, gb)
            devs = xdev + ydev
        else:
            srcs = dsts = (
                grads.at[c, second, xp, rows, a], grads.at[c, first, xm, rows, a],
                grads.at[c, yp, second, rows, b], grads.at[c, ym, first, rows, b],
            )
            devs = xdev + ydev
        return [
            remote(s, d, send.at[c, 4 * k + i], recv.at[c, 4 * k + i], dev)
            for i, (s, d, dev) in enumerate(zip(srcs, dsts, devs))
        ]

    def start(c, k):
        for copy in copies(c, k):
            copy.start()

    def arrived(c, k):
        for copy in copies(c, k):
            copy.wait_recv()

    def f(v):
        return v.astype(F32)

    def forward(c):
        product = jnp.dot(
            toks[...].reshape(8 * 64, toks.shape[2]), weights[c], preferred_element_type=F32
        ).astype(BF16).reshape(4, 4, 32, 2 * ch)
        part[c, 0] = product[:, :, :, :ch]
        part[c, 1] = product[:, :, :, ch:]
        start(c, 0)

    def merge1(c):
        arrived(c, 0)
        part[c, 0, 0:2, xm] = (f(part[c, 0, 0:2, xm]) + f(half1[c, 0, 0])).astype(BF16)
        part[c, 0, 2:4, xp] = (f(part[c, 0, 2:4, xp]) + f(half1[c, 0, 1])).astype(BF16)
        part[c, 1, ym, 0:2] = (f(part[c, 1, ym, 0:2]) + f(half1[c, 1, 0])).astype(BF16)
        part[c, 1, yp, 2:4] = (f(part[c, 1, yp, 2:4]) + f(half1[c, 1, 1])).astype(BF16)
        start(c, 1)

    def total1(c):
        arrived(c, 1)
        sum1[c, 0] = (f(part[c, 0, :, x]) + f(full1[c, 0, 0]) + f(full1[c, 0, 1])).astype(BF16)
        sum1[c, 1] = (f(part[c, 1, y]) + f(full1[c, 1, 0]) + f(full1[c, 1, 1])).astype(BF16)
        start(c, 2)

    def merge2(c):
        arrived(c, 2)
        for i, (m, p) in enumerate(((ym, yp), (xm, xp))):
            sum1[c, i, m, :, 0:hc] = (f(sum1[c, i, m, :, 0:hc]) + f(half2[c, i, 0])).astype(BF16)
            sum1[c, i, p, :, hc:ch] = (f(sum1[c, i, p, :, hc:ch]) + f(half2[c, i, 1])).astype(BF16)
        start(c, 3)

    def activate(c):
        arrived(c, 3)
        cot_copy(c).wait()
        gate_sum = f(sum1[c, 0, y]) + f(full2[c, 0, 0]) + f(full2[c, 0, 1])
        up_sum = f(sum1[c, 1, x]) + f(full2[c, 1, 0]) + f(full2[c, 1, 1])
        sigmoid_gate = jax.nn.sigmoid(gate_sum)
        activated = gate_sum * sigmoid_gate
        cot_f = f(cot_v[c])
        grads[c, y, x, :, 0:ch] = (
            cot_f * up_sum * sigmoid_gate * (1.0 + gate_sum * (1.0 - sigmoid_gate))
        ).astype(BF16)
        grads[c, y, x, :, ch:2 * ch] = (cot_f * activated).astype(BF16)
        start(c, 4)
        hid_v[c] = (activated * up_sum).astype(BF16)
        hid_copy(c).start()

    def forward1(c):
        arrived(c, 4)
        start(c, 5)

    def spread2(c):
        arrived(c, 5)
        start(c, 6)

    def forward2(c):
        arrived(c, 6)
        start(c, 7)

    width = toks.shape[2] // PIECES

    def back(c, n):
        return lax.dot_general(
            grads[c].reshape(512, 2 * ch), weights[c, pl.ds(n * width, width), :],
            (((1,), (1,)), ((), ())), preferred_element_type=F32,
        ).reshape(4, 2, 64, width)

    def backward(c):
        arrived(c, 7)
        for n in range(PIECES):
            acc[n] += back(c, n)

    def masked_forward(c):
        @pl.when(c > 0)
        def _():
            mask(c)

        forward(c)

    stages = (masked_forward, merge1, total1, merge2, activate, forward1, spread2, forward2, backward)
    order = (0, 2, 3, 4, 5, 6, 7, 1, 8)
    steps = chunks + LAGS[8]

    @pl.loop(0, steps - 1)
    def _(step):
        for k in order:
            c = step - LAGS[k]
            last = chunks - 1 if k == 8 else chunks

            @pl.when((c >= 0) & (c < last))
            def _():
                stages[k](c)

    for k in range(1, 8):
        for c in range(max(0, steps - 1 - LAGS[k]), chunks):
            stages[k](c)

    final = chunks - 1
    arrived(final, 7)

    def z_sib(n):
        return remote(zsend.at[n], zsib.at[n], zs.at[9 + n], zr.at[9 + n], sibling)

    base1, base2 = 9 + PIECES, 9 + 3 * PIECES

    def z_half(n):
        return (
            remote(zsend.at[n, z2, lo], zhalf.at[n, 0], zs.at[base1 + 2 * n], zr.at[base1 + 2 * n], left_z),
            remote(zsend.at[n, z2, hi], zhalf.at[n, 1], zs.at[base1 + 2 * n + 1], zr.at[base1 + 2 * n + 1], right_z),
        )

    def z_full(n):
        return (
            remote(zsend.at[n, zm], zfull.at[n, 0], zs.at[base2 + 2 * n], zr.at[base2 + 2 * n], left_z),
            remote(zsend.at[n, zp], zfull.at[n, 1], zs.at[base2 + 2 * n + 1], zr.at[base2 + 2 * n + 1], right_z),
        )

    def out_copy(n):
        return pltpu.make_async_copy(out_v.at[n], grad_out.at[:, pl.ds(n * width, width)], os.at[n])

    def piece_a(n):
        acc[n] += back(final, n)
        zsend[n] = acc[n, :, other].astype(BF16)
        z_sib(n).start()

    def piece_b(n):
        z_sib(n).wait()
        acc[n, :, core] += f(zsib[n])
        zsend[n] = acc[n, :, core].astype(BF16)
        for copy in z_half(n):
            copy.start()

    def piece_c(n):
        for copy in z_half(n):
            copy.wait_recv()
        zsend[n, zm, 0:32] = (acc[n, zm, core, 0:32] + f(zhalf[n, 0])).astype(BF16)
        zsend[n, zp, 32:64] = (acc[n, zp, core, 32:64] + f(zhalf[n, 1])).astype(BF16)
        for copy in z_full(n):
            copy.start()

    def piece_d(n):
        for copy in z_full(n):
            copy.wait_recv()
        out_v[n] = (acc[n, z, core] + f(zfull[n, 0]) + f(zfull[n, 1])).astype(BF16)
        out_copy(n).start()

    for step in range(PIECES + 3):
        for lag, piece in enumerate((piece_a, piece_b, piece_c, piece_d)):
            if 0 <= step - lag < PIECES:
                piece(step - lag)

    for copy in (g_left, g_right, g_sib, f_left, f_right, s_p, s_m, s_2):
        copy.wait_send()
    for n in range(PIECES):
        for copy in z_half(n) + z_full(n):
            copy.wait_send()
        out_copy(n).wait()

    @pl.loop(0, chunks)
    def _(c):
        for k in range(8):
            for copy in copies(c, k):
                copy.wait_send()
        hid_copy(c).wait()


def shards(inputs, gate_weight, up_weight, gate_pattern, up_pattern, cotangent):
    tokens, depth = inputs.shape
    hidden = gate_weight.shape[1]
    chunks = hidden // CHUNK
    ch = CHUNK
    width = depth // PIECES
    any_spec = pl.BlockSpec(memory_space=pl.ANY)
    smem = pl.BlockSpec(memory_space=pltpu.SMEM)
    dma = pltpu.SemaphoreType.DMA
    scratch = [
        pltpu.VMEM((8, tokens, depth), BF16),
        pltpu.VMEM((chunks, depth, 2 * ch), BF16),
        pltpu.VMEM((chunks, 2, 4, 4, 32, ch), BF16),
        pltpu.VMEM((chunks, 2, 2, 2, 32, ch), BF16),
        pltpu.VMEM((chunks, 2, 2, 4, 32, ch), BF16),
        pltpu.VMEM((chunks, 2, 4, 32, ch), BF16),
        pltpu.VMEM((chunks, 2, 2, 32, ch // 2), BF16),
        pltpu.VMEM((chunks, 2, 2, 32, ch), BF16),
        pltpu.VMEM((chunks, 4, 4, 32, 2 * ch), BF16),
        pltpu.VMEM((PIECES, 4, 2, 64, width), F32),
        pltpu.VMEM((PIECES, 4, 64, width), BF16),
        pltpu.VMEM((PIECES, 4, 64, width), BF16),
        pltpu.VMEM((PIECES, 2, 32, width), BF16),
        pltpu.VMEM((PIECES, 2, 64, width), BF16),
        pltpu.VMEM((chunks, 32, ch), BF16),
        pltpu.VMEM((chunks, 32, ch), BF16),
        pltpu.VMEM((PIECES, 64, width), BF16),
        dma((chunks, 32)),
        dma((chunks, 32)),
        dma((9 + 5 * PIECES,)),
        dma((9 + 5 * PIECES,)),
        dma((chunks, 2)),
        dma((chunks,)),
        dma((chunks,)),
        dma((PIECES,)),
    ]
    return pl.pallas_call(
        functools.partial(kernel, chunks),
        out_shape=(
            jax.ShapeDtypeStruct((32, hidden), BF16),
            jax.ShapeDtypeStruct((tokens, depth), BF16),
        ),
        in_specs=[any_spec, any_spec, any_spec, smem, smem, any_spec],
        out_specs=(any_spec, any_spec),
        scratch_shapes=scratch,
        compiler_params=pltpu.CompilerParams(
            collective_id=0, has_side_effects=True, vmem_limit_bytes=58 * 1024 * 1024
        ),
        cost_estimate=pl.CostEstimate(
            flops=4 * 512 * depth * 2 * hidden, bytes_accessed=4 * depth * hidden, transcendentals=32 * hidden
        ),
    )(inputs, gate_weight, up_weight, gate_pattern, up_pattern, cotangent)


def solution(mesh):
    placed = (
        P("col", "row"),
        P("row", "col"),
        P("row", "col"),
        P("row", "col"),
        P("row", "col"),
        P("row", "col"),
    )
    return jax.shard_map(
        shards,
        mesh=mesh,
        in_specs=placed,
        out_specs=(P("row", "col"), P("col", "row")),
        check_vma=False,
    )
```

```python
import functools

import jax
import jax.numpy as jnp
from jax import lax
from jax.experimental import pallas as pl
from jax.experimental.pallas import tpu as pltpu
from jax.sharding import PartitionSpec as P

BLOCK = 128
SIDE = 4
CHUNK = 256
PIECES = 4
LAGS = (0, 4, 8, 12, 16, 20, 24, 28, 32)
F32 = jnp.float32
BF16 = jnp.bfloat16


def kernel(
    chunks, inputs, gate_w, up_w, gate_pat, up_pat, cot, hidden_out, grad_out,
    toks, weights, part, half1, full1, sum1, half2, full2, grads, acc, zsend, zsib, zkeep, zhalf, zfull,
    cot_v, hid_v, out_v, send, recv, zsent, zin, zout, ws, local,
):
    ch = CHUNK
    hc = ch // 2
    row, col = lax.axis_index("row"), lax.axis_index("col")
    y, x = row // SIDE, row % SIDE
    z, core = col // 2, col % 2
    ym, yp, y2 = (y + 3) % SIDE, (y + 1) % SIDE, (y + 2) % SIDE
    xm, xp, x2 = (x + 3) % SIDE, (x + 1) % SIDE, (x + 2) % SIDE
    zm, zp, z2 = (z + 3) % SIDE, (z + 1) % SIDE, (z + 2) % SIDE
    other = 1 - core

    def at(yy, xx):
        return (yy * SIDE + xx, col)

    def atz(zz, cc):
        return (row, zz * 2 + cc)

    left_x, right_x, left_y, right_y = at(y, xm), at(y, xp), at(ym, x), at(yp, x)
    left_z, right_z, sibling = atz(zm, core), atz(zp, core), atz(z, other)

    def remote(src, dst, s, r, dev):
        return pltpu.make_async_remote_copy(
            src_ref=src, dst_ref=dst, send_sem=s, recv_sem=r,
            device_id=dev, device_id_type=pl.DeviceIdType.MESH,
        )

    def weight_copies(c):
        cols = pl.ds(pl.multiple_of(c * ch, ch), ch)
        return (
            pltpu.make_async_copy(gate_w.at[:, cols], weights.at[c, :, pl.ds(0, ch)], ws.at[c]),
            pltpu.make_async_copy(up_w.at[:, cols], weights.at[c, :, pl.ds(ch, ch)], ws.at[c]),
        )

    def cot_copy(c):
        return pltpu.make_async_copy(cot.at[:, pl.ds(pl.multiple_of(c * ch, ch), ch)], cot_v.at[c], local.at[1])

    def hid_copy(c):
        return pltpu.make_async_copy(hid_v.at[c], hidden_out.at[:, pl.ds(pl.multiple_of(c * ch, ch), ch)], local.at[2])

    own_copy = pltpu.make_async_copy(inputs, toks.at[col], local.at[0])
    own_copy.start()

    @pl.loop(0, chunks)
    def _(c):
        for copy in weight_copies(c):
            copy.start()

    @pl.loop(0, chunks)
    def _(c):
        cot_copy(c).start()

    barrier = pltpu.get_barrier_semaphore()
    for dev in (left_x, right_x, left_y, right_y, left_z, right_z, sibling):
        pl.semaphore_signal(barrier, inc=1, device_id=dev, device_id_type=pl.DeviceIdType.MESH)
    def all_landed(ref, sem):
        remote(ref, ref, sem, sem, sibling).wait_recv()

    def all_left(ref, sem):
        remote(ref, ref, sem, sem, sibling).wait_send()

    def mask(c):
        pltpu.make_async_copy(weights.at[c], weights.at[c], ws.at[c]).wait()
        for which, pat in enumerate((gate_pat, up_pat)):
            for i in range(weights.shape[1] // BLOCK):
                for j in range(ch // BLOCK):
                    flag = pat[i, c * (ch // BLOCK) + j].astype(F32)
                    rows, cols = pl.ds(i * BLOCK, BLOCK), pl.ds(which * ch + j * BLOCK, BLOCK)
                    weights[c, rows, cols] = (weights[c, rows, cols].astype(F32) * flag).astype(BF16)

    def mask_some(part_of):
        pl.loop(part_of * chunks // 3, (part_of + 1) * chunks // 3)(mask)

    mask_some(0)
    pl.semaphore_wait(barrier, 7)

    mine, from_m, from_p, from_2 = z * 2 + core, zm * 2 + core, zp * 2 + core, z2 * 2 + core
    lo, hi = pl.ds(0, 32), pl.ds(32, 32)

    def spread(src, dst, k, dev):
        return remote(src, dst, zsent.at[0], zin.at[k], dev)

    def from_input(rows, k, dev):
        return spread(inputs.at[rows], toks.at[mine, rows], k, dev)

    def onward(block, rows, k, dev):
        return spread(toks.at[block, rows], toks.at[block, rows], k, dev)

    whole = pl.ds(0, 64)
    to_left_hi, to_right_lo = from_input(hi, 0, left_z), from_input(lo, 2, right_z)
    to_left_lo, to_right_hi = from_input(lo, 1, left_z), from_input(hi, 3, right_z)
    to_sibling = from_input(whole, 4, sibling)
    for copy in (to_left_hi, to_right_lo, to_left_lo, to_right_hi, to_sibling):
        copy.start()
    acc[...] = jnp.zeros(acc.shape, F32)
    mask_some(1)
    on_left, on_right = onward(from_p, hi, 5, left_z), onward(from_m, lo, 6, right_z)
    to_left_hi.wait_recv()
    on_left.start()
    to_right_lo.wait_recv()
    on_right.start()
    share_p, share_m = onward(from_p, whole, 7, sibling), onward(from_m, whole, 8, sibling)
    share_2hi, share_2lo = onward(from_2, hi, 9, sibling), onward(from_2, lo, 10, sibling)
    to_left_lo.wait_recv()
    share_p.start()
    to_right_hi.wait_recv()
    share_m.start()
    mask_some(2)
    on_left.wait_recv()
    share_2hi.start()
    on_right.wait_recv()
    share_2lo.start()
    own_copy.wait()
    pltpu.make_async_copy(cot_v, cot_v, local.at[1]).wait()
    for copy in (to_sibling, share_p, share_m, share_2hi, share_2lo):
        copy.wait_recv()

    def copies(c, k):
        a, b = pl.ds(0, ch), pl.ds(ch, ch)
        al, ar, bl, br = pl.ds(0, hc), pl.ds(hc, hc), pl.ds(ch, hc), pl.ds(ch + hc, hc)
        first, second, every = pl.ds(0, 2), pl.ds(2, 2), pl.ds(0, 4)
        rows = pl.ds(0, 32)
        xdev, ydev = (left_x, right_x), (left_y, right_y)
        if k == 0:
            srcs = (part.at[c, 0, first, x2], part.at[c, 0, second, x2], part.at[c, 1, y2, first], part.at[c, 1, y2, second])
            dsts = tuple(half1.at[c, i // 2, i % 2] for i in range(4))
            devs = xdev + ydev
        elif k == 1:
            srcs = (part.at[c, 0, every, xm], part.at[c, 0, every, xp], part.at[c, 1, ym], part.at[c, 1, yp])
            dsts = tuple(full1.at[c, i // 2, i % 2] for i in range(4))
            devs = xdev + ydev
        elif k == 2:
            srcs = (
                sum1.at[c, 0, y2, rows, al], sum1.at[c, 0, y2, rows, ar],
                sum1.at[c, 1, x2, rows, al], sum1.at[c, 1, x2, rows, ar],
            )
            dsts = tuple(half2.at[c, i // 2, i % 2] for i in range(4))
            devs = ydev + xdev
        elif k == 3:
            srcs = (sum1.at[c, 0, ym], sum1.at[c, 0, yp], sum1.at[c, 1, xm], sum1.at[c, 1, xp])
            dsts = tuple(full2.at[c, i // 2, i % 2] for i in range(4))
            devs = ydev + xdev
        elif k == 4:
            ga, gb = grads.at[c, y, x, rows, a], grads.at[c, y, x, rows, b]
            srcs = dsts = (ga, ga, gb, gb)
            devs = ydev + xdev
        elif k == 5:
            srcs = dsts = (
                grads.at[c, yp, x, rows, ar], grads.at[c, ym, x, rows, al],
                grads.at[c, y, xp, rows, br], grads.at[c, y, xm, rows, bl],
            )
            devs = ydev + xdev
        elif k == 6:
            ga, gb = grads.at[c, every, x, rows, a], grads.at[c, y, every, rows, b]
            srcs = dsts = (ga, ga, gb, gb)
            devs = xdev + ydev
        else:
            srcs = dsts = (
                grads.at[c, second, xp, rows, a], grads.at[c, first, xm, rows, a],
                grads.at[c, yp, second, rows, b], grads.at[c, ym, first, rows, b],
            )
            devs = xdev + ydev
        return [
            remote(s, d, send.at[k], recv.at[c, k], dev)
            for s, d, dev in zip(srcs, dsts, devs)
        ]

    def start(c, k):
        for copy in copies(c, k):
            copy.start()

    sizes = (half1, full1, half2, full2, full2, half2, full1, half1)

    def arrived(c, k):
        all_landed(sizes[k].at[c], recv.at[c, k])

    def f(v):
        return v.astype(F32)

    def forward(c):
        product = jnp.dot(
            toks[...].reshape(8 * 64, toks.shape[2]), weights[c], preferred_element_type=F32
        ).astype(BF16).reshape(4, 4, 32, 2 * ch)
        part[c, 0] = product[:, :, :, :ch]
        part[c, 1] = product[:, :, :, ch:]
        start(c, 0)

    def merge1(c):
        arrived(c, 0)
        part[c, 0, 0:2, xm] = (f(part[c, 0, 0:2, xm]) + f(half1[c, 0, 0])).astype(BF16)
        part[c, 0, 2:4, xp] = (f(part[c, 0, 2:4, xp]) + f(half1[c, 0, 1])).astype(BF16)
        part[c, 1, ym, 0:2] = (f(part[c, 1, ym, 0:2]) + f(half1[c, 1, 0])).astype(BF16)
        part[c, 1, yp, 2:4] = (f(part[c, 1, yp, 2:4]) + f(half1[c, 1, 1])).astype(BF16)
        start(c, 1)

    def total1(c):
        arrived(c, 1)
        sum1[c, 0] = (f(part[c, 0, :, x]) + f(full1[c, 0, 0]) + f(full1[c, 0, 1])).astype(BF16)
        sum1[c, 1] = (f(part[c, 1, y]) + f(full1[c, 1, 0]) + f(full1[c, 1, 1])).astype(BF16)
        start(c, 2)

    def merge2(c):
        arrived(c, 2)
        for i, (m, p) in enumerate(((ym, yp), (xm, xp))):
            sum1[c, i, m, :, 0:hc] = (f(sum1[c, i, m, :, 0:hc]) + f(half2[c, i, 0])).astype(BF16)
            sum1[c, i, p, :, hc:ch] = (f(sum1[c, i, p, :, hc:ch]) + f(half2[c, i, 1])).astype(BF16)
        start(c, 3)

    def activate(c):
        arrived(c, 3)
        gate_sum = f(sum1[c, 0, y]) + f(full2[c, 0, 0]) + f(full2[c, 0, 1])
        up_sum = f(sum1[c, 1, x]) + f(full2[c, 1, 0]) + f(full2[c, 1, 1])
        sigmoid_gate = jax.nn.sigmoid(gate_sum)
        activated = gate_sum * sigmoid_gate
        cot_f = f(cot_v[c])
        grads[c, y, x, :, 0:ch] = (
            cot_f * up_sum * sigmoid_gate * (1.0 + gate_sum * (1.0 - sigmoid_gate))
        ).astype(BF16)
        grads[c, y, x, :, ch:2 * ch] = (cot_f * activated).astype(BF16)
        start(c, 4)
        hid_v[c] = (activated * up_sum).astype(BF16)
        hid_copy(c).start()

    def forward1(c):
        arrived(c, 4)
        start(c, 5)

    def spread2(c):
        arrived(c, 5)
        start(c, 6)

    def forward2(c):
        arrived(c, 6)
        start(c, 7)

    width = toks.shape[2] // PIECES

    def back(c, n):
        return lax.dot_general(
            grads[c].reshape(512, 2 * ch), weights[c, pl.ds(n * width, width), :],
            (((1,), (1,)), ((), ())), preferred_element_type=F32,
        ).reshape(4, 2, 64, width)

    def backward(c):
        arrived(c, 7)
        for n in range(PIECES):
            acc[n] += back(c, n)

    stages = (forward, merge1, total1, merge2, activate, forward1, spread2, forward2, backward)
    order = (7, 6, 5, 4, 3, 2, 1, 0, 8)
    steps = chunks + LAGS[8]

    @pl.loop(0, steps - 1)
    def _(step):
        for k in order:
            c = step - LAGS[k]
            last = chunks - 1 if k == 8 else chunks

            @pl.when((c >= 0) & (c < last))
            def _():
                stages[k](c)

    for k in range(1, 8):
        for c in range(max(0, steps - 1 - LAGS[k]), chunks):
            stages[k](c)

    final = chunks - 1
    arrived(final, 7)

    def z_send(src, dst, k, n, dev):
        return remote(src, dst, zsent.at[1], zout.at[k, n], dev)

    def z_sib(n):
        return z_send(zsend.at[n], zsib.at[n], 0, n, sibling)

    def z_half(n):
        return (
            z_send(zkeep.at[n, z2, lo], zhalf.at[n, 0], 1, n, left_z),
            z_send(zkeep.at[n, z2, hi], zhalf.at[n, 1], 1, n, right_z),
        )

    def z_full(n):
        return (
            z_send(zkeep.at[n, zm], zfull.at[n, 0], 2, n, left_z),
            z_send(zkeep.at[n, zp], zfull.at[n, 1], 2, n, right_z),
        )

    def out_copy(n):
        return pltpu.make_async_copy(out_v.at[n], grad_out.at[:, pl.ds(n * width, width)], local.at[3])

    def piece_a(n):
        acc[n] += back(final, n)
        zsend[n] = acc[n, :, other].astype(BF16)
        z_sib(n).start()

    def piece_b(n):
        all_landed(zsib.at[n], zout.at[0, n])
        total = acc[n, :, core] + f(zsib[n])
        acc[n, :, core] = total
        zkeep[n] = total.astype(BF16)
        for copy in z_half(n):
            copy.start()

    def piece_c(n):
        all_landed(zhalf.at[n], zout.at[1, n])
        zkeep[n, zm, 0:32] = (acc[n, zm, core, 0:32] + f(zhalf[n, 0])).astype(BF16)
        zkeep[n, zp, 32:64] = (acc[n, zp, core, 32:64] + f(zhalf[n, 1])).astype(BF16)
        for copy in z_full(n):
            copy.start()

    def piece_d(n):
        all_landed(zfull.at[n], zout.at[2, n])
        out_v[n] = (acc[n, z, core] + f(zfull[n, 0]) + f(zfull[n, 1])).astype(BF16)
        out_copy(n).start()

    for step in range(PIECES + 3):
        for lag, piece in enumerate((piece_a, piece_b, piece_c, piece_d)):
            if 0 <= step - lag < PIECES:
                piece(step - lag)

    for k in range(8):
        all_left(sizes[k], send.at[k])
    for k in range(2):
        all_left(toks.at[pl.ds(0, 7)], zsent.at[k])
    pltpu.make_async_copy(hid_v, hid_v, local.at[2]).wait()
    pltpu.make_async_copy(out_v, out_v, local.at[3]).wait()


def shards(inputs, gate_weight, up_weight, gate_pattern, up_pattern, cotangent):
    tokens, depth = inputs.shape
    hidden = gate_weight.shape[1]
    chunks = hidden // CHUNK
    ch = CHUNK
    width = depth // PIECES
    any_spec = pl.BlockSpec(memory_space=pl.ANY)
    smem = pl.BlockSpec(memory_space=pltpu.SMEM)
    dma = pltpu.SemaphoreType.DMA
    scratch = [
        pltpu.VMEM((8, tokens, depth), BF16),
        pltpu.VMEM((chunks, depth, 2 * ch), BF16),
        pltpu.VMEM((chunks, 2, 4, 4, 32, ch), BF16),
        pltpu.VMEM((chunks, 2, 2, 2, 32, ch), BF16),
        pltpu.VMEM((chunks, 2, 2, 4, 32, ch), BF16),
        pltpu.VMEM((chunks, 2, 4, 32, ch), BF16),
        pltpu.VMEM((chunks, 2, 2, 32, ch // 2), BF16),
        pltpu.VMEM((chunks, 2, 2, 32, ch), BF16),
        pltpu.VMEM((chunks, 4, 4, 32, 2 * ch), BF16),
        pltpu.VMEM((PIECES, 4, 2, 64, width), F32),
        pltpu.VMEM((PIECES, 4, 64, width), BF16),
        pltpu.VMEM((PIECES, 4, 64, width), BF16),
        pltpu.VMEM((PIECES, 4, 64, width), BF16),
        pltpu.VMEM((PIECES, 2, 32, width), BF16),
        pltpu.VMEM((PIECES, 2, 64, width), BF16),
        pltpu.VMEM((chunks, 32, ch), BF16),
        pltpu.VMEM((chunks, 32, ch), BF16),
        pltpu.VMEM((PIECES, 64, width), BF16),
        dma((8,)),
        dma((chunks, 8)),
        dma((2,)),
        dma((11,)),
        dma((3, PIECES)),
        dma((chunks,)),
        dma((4,)),
    ]
    return pl.pallas_call(
        functools.partial(kernel, chunks),
        out_shape=(
            jax.ShapeDtypeStruct((32, hidden), BF16),
            jax.ShapeDtypeStruct((tokens, depth), BF16),
        ),
        in_specs=[any_spec, any_spec, any_spec, smem, smem, any_spec],
        out_specs=(any_spec, any_spec),
        scratch_shapes=scratch,
        compiler_params=pltpu.CompilerParams(
            collective_id=0, has_side_effects=True, vmem_limit_bytes=58 * 1024 * 1024
        ),
        cost_estimate=pl.CostEstimate(
            flops=4 * 512 * depth * 2 * hidden, bytes_accessed=4 * depth * hidden, transcendentals=32 * hidden
        ),
    )(inputs, gate_weight, up_weight, gate_pattern, up_pattern, cotangent)


def solution(mesh):
    placed = (
        P("col", "row"),
        P("row", "col"),
        P("row", "col"),
        P("row", "col"),
        P("row", "col"),
        P("row", "col"),
    )
    return jax.shard_map(
        shards,
        mesh=mesh,
        in_specs=placed,
        out_specs=(P("row", "col"), P("col", "row")),
        check_vma=False,
    )
```

```python
import functools

import jax
import jax.numpy as jnp
from jax import lax
from jax.experimental import pallas as pl
from jax.experimental.pallas import tpu as pltpu
from jax.sharding import PartitionSpec as P

BLOCK = 128
SIDE = 4
CHUNK = 256
PIECES = 4
LAGS = (0, 4, 8, 12, 16, 20, 24, 28, 32)
F32 = jnp.float32
BF16 = jnp.bfloat16


def kernel(
    chunks, inputs, gate_w, up_w, gate_pat, up_pat, cot, hidden_out, grad_out,
    toks, weights, part, half1, full1, sum1, half2, full2, grads, acc, zsend, zsib, zkeep, zhalf, zfull,
    cot_v, hid_v, out_v, send, recv, zsent, zin, zout, ws, local,
):
    ch = CHUNK
    hc = ch // 2
    row, col = lax.axis_index("row"), lax.axis_index("col")
    y, x = row // SIDE, row % SIDE
    z, core = col // 2, col % 2
    ym, yp, y2 = (y + 3) % SIDE, (y + 1) % SIDE, (y + 2) % SIDE
    xm, xp, x2 = (x + 3) % SIDE, (x + 1) % SIDE, (x + 2) % SIDE
    zm, zp, z2 = (z + 3) % SIDE, (z + 1) % SIDE, (z + 2) % SIDE
    other = 1 - core

    def at(yy, xx):
        return (yy * SIDE + xx, col)

    def atz(zz, cc):
        return (row, zz * 2 + cc)

    left_x, right_x, left_y, right_y = at(y, xm), at(y, xp), at(ym, x), at(yp, x)
    left_z, right_z, sibling = atz(zm, core), atz(zp, core), atz(z, other)

    def remote(src, dst, s, r, dev):
        return pltpu.make_async_remote_copy(
            src_ref=src, dst_ref=dst, send_sem=s, recv_sem=r,
            device_id=dev, device_id_type=pl.DeviceIdType.MESH,
        )

    def weight_copies(c):
        cols = pl.ds(pl.multiple_of(c * ch, ch), ch)
        return (
            pltpu.make_async_copy(gate_w.at[:, cols], weights.at[c, :, pl.ds(0, ch)], ws.at[c]),
            pltpu.make_async_copy(up_w.at[:, cols], weights.at[c, :, pl.ds(ch, ch)], ws.at[c]),
        )

    def cot_copy(c):
        return pltpu.make_async_copy(cot.at[:, pl.ds(pl.multiple_of(c * ch, ch), ch)], cot_v.at[c], local.at[1])

    def hid_copy(c):
        return pltpu.make_async_copy(hid_v.at[c], hidden_out.at[:, pl.ds(pl.multiple_of(c * ch, ch), ch)], local.at[2])

    own_copy = pltpu.make_async_copy(inputs, toks.at[col], local.at[0])
    own_copy.start()

    @pl.loop(0, chunks)
    def _(c):
        for copy in weight_copies(c):
            copy.start()

    @pl.loop(0, chunks)
    def _(c):
        cot_copy(c).start()

    barrier = pltpu.get_barrier_semaphore()
    for dev in (left_x, right_x, left_y, right_y, left_z, right_z, sibling):
        pl.semaphore_signal(barrier, inc=1, device_id=dev, device_id_type=pl.DeviceIdType.MESH)
    def all_landed(ref, sem):
        remote(ref, ref, sem, sem, sibling).wait_recv()

    def all_left(ref, sem):
        remote(ref, ref, sem, sem, sibling).wait_send()

    def mask(c):
        pltpu.make_async_copy(weights.at[c], weights.at[c], ws.at[c]).wait()
        for which, pat in enumerate((gate_pat, up_pat)):
            for i in range(weights.shape[1] // BLOCK):
                for j in range(ch // BLOCK):
                    flag = pat[i, c * (ch // BLOCK) + j].astype(F32)
                    rows, cols = pl.ds(i * BLOCK, BLOCK), pl.ds(which * ch + j * BLOCK, BLOCK)
                    weights[c, rows, cols] = (weights[c, rows, cols].astype(F32) * flag).astype(BF16)

    def mask_some(part_of):
        pl.loop(part_of * chunks // 3, (part_of + 1) * chunks // 3)(mask)

    mask_some(0)
    pl.semaphore_wait(barrier, 7)

    mine, from_m, from_p, from_2 = z * 2 + core, zm * 2 + core, zp * 2 + core, z2 * 2 + core
    lo, hi = pl.ds(0, 32), pl.ds(32, 32)

    def spread(src, dst, k, dev):
        return remote(src, dst, zsent.at[0], zin.at[k], dev)

    def from_input(rows, k, dev):
        return spread(inputs.at[rows], toks.at[mine, rows], k, dev)

    def onward(block, rows, k, dev):
        return spread(toks.at[block, rows], toks.at[block, rows], k, dev)

    whole = pl.ds(0, 64)
    to_left_hi, to_right_lo = from_input(hi, 0, left_z), from_input(lo, 2, right_z)
    to_left_lo, to_right_hi = from_input(lo, 1, left_z), from_input(hi, 3, right_z)
    to_sibling = from_input(whole, 4, sibling)
    for copy in (to_left_hi, to_right_lo, to_left_lo, to_right_hi, to_sibling):
        copy.start()
    acc[...] = jnp.zeros(acc.shape, F32)
    mask_some(1)
    on_left, on_right = onward(from_p, hi, 5, left_z), onward(from_m, lo, 6, right_z)
    to_left_hi.wait_recv()
    on_left.start()
    to_right_lo.wait_recv()
    on_right.start()
    share_p, share_m = onward(from_p, whole, 7, sibling), onward(from_m, whole, 8, sibling)
    share_2hi, share_2lo = onward(from_2, hi, 9, sibling), onward(from_2, lo, 10, sibling)
    to_left_lo.wait_recv()
    share_p.start()
    to_right_hi.wait_recv()
    share_m.start()
    mask_some(2)
    on_left.wait_recv()
    share_2hi.start()
    on_right.wait_recv()
    share_2lo.start()
    own_copy.wait()
    pltpu.make_async_copy(cot_v, cot_v, local.at[1]).wait()
    for copy in (to_sibling, share_p, share_m, share_2hi, share_2lo):
        copy.wait_recv()

    def copies(c, k):
        a, b = pl.ds(0, ch), pl.ds(ch, ch)
        al, ar, bl, br = pl.ds(0, hc), pl.ds(hc, hc), pl.ds(ch, hc), pl.ds(ch + hc, hc)
        first, second, every = pl.ds(0, 2), pl.ds(2, 2), pl.ds(0, 4)
        rows = pl.ds(0, 32)
        xdev, ydev = (left_x, right_x), (left_y, right_y)
        if k == 0:
            srcs = (part.at[c, 0, first, x2], part.at[c, 0, second, x2], part.at[c, 1, y2, first], part.at[c, 1, y2, second])
            dsts = tuple(half1.at[c, i // 2, i % 2] for i in range(4))
            devs = xdev + ydev
        elif k == 1:
            srcs = (part.at[c, 0, every, xm], part.at[c, 0, every, xp], part.at[c, 1, ym], part.at[c, 1, yp])
            dsts = tuple(full1.at[c, i // 2, i % 2] for i in range(4))
            devs = xdev + ydev
        elif k == 2:
            srcs = (
                sum1.at[c, 0, y2, rows, al], sum1.at[c, 0, y2, rows, ar],
                sum1.at[c, 1, x2, rows, al], sum1.at[c, 1, x2, rows, ar],
            )
            dsts = tuple(half2.at[c, i // 2, i % 2] for i in range(4))
            devs = ydev + xdev
        elif k == 3:
            srcs = (sum1.at[c, 0, ym], sum1.at[c, 0, yp], sum1.at[c, 1, xm], sum1.at[c, 1, xp])
            dsts = tuple(full2.at[c, i // 2, i % 2] for i in range(4))
            devs = ydev + xdev
        elif k == 4:
            ga, gb = grads.at[c, y, x, rows, a], grads.at[c, y, x, rows, b]
            srcs = dsts = (ga, ga, gb, gb)
            devs = ydev + xdev
        elif k == 5:
            srcs = dsts = (
                grads.at[c, yp, x, rows, ar], grads.at[c, ym, x, rows, al],
                grads.at[c, y, xp, rows, br], grads.at[c, y, xm, rows, bl],
            )
            devs = ydev + xdev
        elif k == 6:
            ga, gb = grads.at[c, every, x, rows, a], grads.at[c, y, every, rows, b]
            srcs = dsts = (ga, ga, gb, gb)
            devs = xdev + ydev
        else:
            srcs = dsts = (
                grads.at[c, second, xp, rows, a], grads.at[c, first, xm, rows, a],
                grads.at[c, yp, second, rows, b], grads.at[c, ym, first, rows, b],
            )
            devs = xdev + ydev
        return [
            remote(s, d, send.at[k], recv.at[c, k], dev)
            for s, d, dev in zip(srcs, dsts, devs)
        ]

    def start(c, k):
        for copy in copies(c, k):
            copy.start()

    sizes = (half1, full1, half2, full2, full2, half2, full1, half1)

    def arrived(c, k):
        all_landed(sizes[k].at[c], recv.at[c, k])

    def f(v):
        return v.astype(F32)

    def forward(c):
        product = jnp.dot(
            toks[...].reshape(8 * 64, toks.shape[2]), weights[c], preferred_element_type=F32
        ).astype(BF16).reshape(4, 4, 32, 2 * ch)
        part[c, 0] = product[:, :, :, :ch]
        part[c, 1] = product[:, :, :, ch:]
        start(c, 0)

    def merge1(c):
        arrived(c, 0)
        part[c, 0, 0:2, xm] = (f(part[c, 0, 0:2, xm]) + f(half1[c, 0, 0])).astype(BF16)
        part[c, 0, 2:4, xp] = (f(part[c, 0, 2:4, xp]) + f(half1[c, 0, 1])).astype(BF16)
        part[c, 1, ym, 0:2] = (f(part[c, 1, ym, 0:2]) + f(half1[c, 1, 0])).astype(BF16)
        part[c, 1, yp, 2:4] = (f(part[c, 1, yp, 2:4]) + f(half1[c, 1, 1])).astype(BF16)
        start(c, 1)

    def total1(c):
        arrived(c, 1)
        sum1[c, 0] = (f(part[c, 0, :, x]) + f(full1[c, 0, 0]) + f(full1[c, 0, 1])).astype(BF16)
        sum1[c, 1] = (f(part[c, 1, y]) + f(full1[c, 1, 0]) + f(full1[c, 1, 1])).astype(BF16)
        start(c, 2)

    def merge2(c):
        arrived(c, 2)
        for i, (m, p) in enumerate(((ym, yp), (xm, xp))):
            sum1[c, i, m, :, 0:hc] = (f(sum1[c, i, m, :, 0:hc]) + f(half2[c, i, 0])).astype(BF16)
            sum1[c, i, p, :, hc:ch] = (f(sum1[c, i, p, :, hc:ch]) + f(half2[c, i, 1])).astype(BF16)
        start(c, 3)

    def activate(c):
        arrived(c, 3)
        gate_sum = f(sum1[c, 0, y]) + f(full2[c, 0, 0]) + f(full2[c, 0, 1])
        up_sum = f(sum1[c, 1, x]) + f(full2[c, 1, 0]) + f(full2[c, 1, 1])
        sigmoid_gate = jax.nn.sigmoid(gate_sum)
        activated = gate_sum * sigmoid_gate
        cot_f = f(cot_v[c])
        grads[c, y, x, :, 0:ch] = (
            cot_f * up_sum * sigmoid_gate * (1.0 + gate_sum * (1.0 - sigmoid_gate))
        ).astype(BF16)
        grads[c, y, x, :, ch:2 * ch] = (cot_f * activated).astype(BF16)
        start(c, 4)
        hid_v[c] = (activated * up_sum).astype(BF16)
        hid_copy(c).start()

    def forward1(c):
        arrived(c, 4)
        start(c, 5)

    def spread2(c):
        arrived(c, 5)
        start(c, 6)

    def forward2(c):
        arrived(c, 6)
        start(c, 7)

    width = toks.shape[2] // PIECES

    def back(c, n):
        return lax.dot_general(
            grads[c].reshape(512, 2 * ch), weights[c, pl.ds(n * width, width), :],
            (((1,), (1,)), ((), ())), preferred_element_type=F32,
        ).reshape(4, 2, 64, width)

    def backward(c):
        arrived(c, 7)
        for n in range(PIECES):
            acc[n] += back(c, n)

    stages = (forward, merge1, total1, merge2, activate, forward1, spread2, forward2, backward)
    order = (7, 6, 5, 4, 3, 2, 1, 0, 8)
    steps = chunks + LAGS[8]

    @pl.loop(0, steps - 1)
    def _(step):
        for k in order:
            c = step - LAGS[k]
            last = chunks - 1 if k == 8 else chunks

            @pl.when((c >= 0) & (c < last))
            def _():
                stages[k](c)

    for k in range(1, 8):
        for c in range(max(0, steps - 1 - LAGS[k]), chunks):
            stages[k](c)

    final = chunks - 1
    arrived(final, 7)

    def z_send(src, dst, k, n, dev):
        return remote(src, dst, zsent.at[1], zout.at[k, n], dev)

    def z_sib(n):
        return z_send(zsend.at[n], zsib.at[n], 0, n, sibling)

    def z_half(n):
        return (
            z_send(zkeep.at[n, z2, lo], zhalf.at[n, 0], 1, n, left_z),
            z_send(zkeep.at[n, z2, hi], zhalf.at[n, 1], 1, n, right_z),
        )

    def z_full(n):
        return (
            z_send(zkeep.at[n, zm], zfull.at[n, 0], 2, n, left_z),
            z_send(zkeep.at[n, zp], zfull.at[n, 1], 2, n, right_z),
        )

    def out_copy(n):
        return pltpu.make_async_copy(out_v.at[n], grad_out.at[:, pl.ds(n * width, width)], local.at[3])

    def piece_a(n):
        acc[n] += back(final, n)
        zsend[n] = acc[n, :, other].astype(BF16)
        z_sib(n).start()

    def piece_b(n):
        all_landed(zsib.at[n], zout.at[0, n])
        total = acc[n, :, core] + f(zsib[n])
        acc[n, :, core] = total
        zkeep[n] = total.astype(BF16)
        for copy in z_half(n):
            copy.start()

    def piece_c(n):
        all_landed(zhalf.at[n], zout.at[1, n])
        zkeep[n, zm, 0:32] = (acc[n, zm, core, 0:32] + f(zhalf[n, 0])).astype(BF16)
        zkeep[n, zp, 32:64] = (acc[n, zp, core, 32:64] + f(zhalf[n, 1])).astype(BF16)
        for copy in z_full(n):
            copy.start()

    def piece_d(n):
        all_landed(zfull.at[n], zout.at[2, n])
        out_v[n] = (acc[n, z, core] + f(zfull[n, 0]) + f(zfull[n, 1])).astype(BF16)
        out_copy(n).start()

    for piece in (piece_a, piece_b, piece_c, piece_d):
        for n in range(PIECES):
            piece(n)

    for k in range(8):
        all_left(sizes[k], send.at[k])
    for k in range(2):
        all_left(toks.at[pl.ds(0, 7)], zsent.at[k])
    pltpu.make_async_copy(hid_v, hid_v, local.at[2]).wait()
    pltpu.make_async_copy(out_v, out_v, local.at[3]).wait()


def hand_over(hidden, grad, hidden_out, grad_out):
    hidden_out[...] = hidden[...]
    grad_out[...] = grad[...]


def shards(inputs, gate_weight, up_weight, gate_pattern, up_pattern, cotangent):
    tokens, depth = inputs.shape
    hidden = gate_weight.shape[1]
    chunks = hidden // CHUNK
    ch = CHUNK
    width = depth // PIECES
    any_spec = pl.BlockSpec(memory_space=pl.ANY)
    smem = pl.BlockSpec(memory_space=pltpu.SMEM)
    dma = pltpu.SemaphoreType.DMA
    scratch = [
        pltpu.VMEM((8, tokens, depth), BF16),
        pltpu.VMEM((chunks, depth, 2 * ch), BF16),
        pltpu.VMEM((chunks, 2, 4, 4, 32, ch), BF16),
        pltpu.VMEM((chunks, 2, 2, 2, 32, ch), BF16),
        pltpu.VMEM((chunks, 2, 2, 4, 32, ch), BF16),
        pltpu.VMEM((chunks, 2, 4, 32, ch), BF16),
        pltpu.VMEM((chunks, 2, 2, 32, ch // 2), BF16),
        pltpu.VMEM((chunks, 2, 2, 32, ch), BF16),
        pltpu.VMEM((chunks, 4, 4, 32, 2 * ch), BF16),
        pltpu.VMEM((PIECES, 4, 2, 64, width), F32),
        pltpu.VMEM((PIECES, 4, 64, width), BF16),
        pltpu.VMEM((PIECES, 4, 64, width), BF16),
        pltpu.VMEM((PIECES, 4, 64, width), BF16),
        pltpu.VMEM((PIECES, 2, 32, width), BF16),
        pltpu.VMEM((PIECES, 2, 64, width), BF16),
        pltpu.VMEM((chunks, 32, ch), BF16),
        pltpu.VMEM((chunks, 32, ch), BF16),
        pltpu.VMEM((PIECES, 64, width), BF16),
        dma((8,)),
        dma((chunks, 8)),
        dma((2,)),
        dma((11,)),
        dma((3, PIECES)),
        dma((chunks,)),
        dma((4,)),
    ]
    results = pl.pallas_call(
        functools.partial(kernel, chunks),
        out_shape=(
            jax.ShapeDtypeStruct((32, hidden), BF16),
            jax.ShapeDtypeStruct((tokens, depth), BF16),
        ),
        in_specs=[any_spec, any_spec, any_spec, smem, smem, any_spec],
        out_specs=(any_spec, any_spec),
        scratch_shapes=scratch,
        compiler_params=pltpu.CompilerParams(
            collective_id=0, has_side_effects=True, vmem_limit_bytes=58 * 1024 * 1024
        ),
        cost_estimate=pl.CostEstimate(
            flops=4 * 512 * depth * 2 * hidden, bytes_accessed=4 * depth * hidden, transcendentals=32 * hidden
        ),
    )(inputs, gate_weight, up_weight, gate_pattern, up_pattern, cotangent)
    return pl.pallas_call(
        hand_over,
        out_shape=tuple(jax.ShapeDtypeStruct(r.shape, r.dtype) for r in results),
        in_specs=[pl.BlockSpec(memory_space=pltpu.VMEM)] * 2,
        out_specs=(pl.BlockSpec(memory_space=pltpu.VMEM),) * 2,
    )(*results)


def solution(mesh):
    placed = (
        P("col", "row"),
        P("row", "col"),
        P("row", "col"),
        P("row", "col"),
        P("row", "col"),
        P("row", "col"),
    )
    return jax.shard_map(
        shards,
        mesh=mesh,
        in_specs=placed,
        out_specs=(P("row", "col"), P("col", "row")),
        check_vma=False,
    )
```

```python
import functools

import jax
import jax.numpy as jnp
from jax import lax
from jax.experimental import pallas as pl
from jax.experimental.pallas import tpu as pltpu
from jax.sharding import PartitionSpec as P

BLOCK = 128
SIDE = 4
CHUNK = 256
GATHER_AT = (5, 9)
SUM_AFTER = (0, 2, 9)
HALF = 16
PIECES = 2
LAGS = (0, 5, 10, 15, 20, 25, 30, 35, 40)
F32 = jnp.float32
BF16 = jnp.bfloat16


def kernel(
    chunks, inputs, gate_w, up_w, gate_pat, up_pat, cot, hidden_out, grad_out,
    toks, weights, part, half1, full1, sum1, half2, full2, grads, acc, zsend, zsib, zkeep, zfull,
    cot_v, hid_v, out_v, send, recv, zsent, zin, zout, ws, local,
):
    ch = CHUNK
    hc = ch // 2
    row, col = lax.axis_index("row"), lax.axis_index("col")
    y, x = row // SIDE, row % SIDE
    z, core = col // 2, col % 2
    ym, yp, y2 = (y + 3) % SIDE, (y + 1) % SIDE, (y + 2) % SIDE
    xm, xp, x2 = (x + 3) % SIDE, (x + 1) % SIDE, (x + 2) % SIDE
    zm, zp, z2 = (z + 3) % SIDE, (z + 1) % SIDE, (z + 2) % SIDE
    other = 1 - core

    def at(yy, xx):
        return (yy * SIDE + xx, col)

    def atz(zz, cc):
        return (row, zz * 2 + cc)

    left_x, right_x, left_y, right_y = at(y, xm), at(y, xp), at(ym, x), at(yp, x)
    left_z, right_z, far_z, sibling = atz(zm, core), atz(zp, core), atz(z2, core), atz(z, other)

    def remote(src, dst, s, r, dev):
        return pltpu.make_async_remote_copy(
            src_ref=src, dst_ref=dst, send_sem=s, recv_sem=r,
            device_id=dev, device_id_type=pl.DeviceIdType.MESH,
        )

    def weight_copies(c):
        cols = pl.ds(pl.multiple_of(c * ch, ch), ch)
        return (
            pltpu.make_async_copy(gate_w.at[:, cols], weights.at[c, :, pl.ds(0, ch)], ws.at[c]),
            pltpu.make_async_copy(up_w.at[:, cols], weights.at[c, :, pl.ds(ch, ch)], ws.at[c]),
        )

    units = 2 * chunks

    def half_of(u):
        return lax.div(u, chunks)

    def chunk_of(u):
        return lax.rem(u, chunks)

    def strip(ref, u):
        rows = pl.ds(pl.multiple_of(half_of(u) * HALF, HALF), HALF)
        return ref.at[rows, pl.ds(pl.multiple_of(chunk_of(u) * ch, ch), ch)]

    def cot_copy(c):
        return pltpu.make_async_copy(strip(cot, c), cot_v.at[c], local.at[1])

    def hid_copy(c):
        return pltpu.make_async_copy(hid_v.at[c], strip(hidden_out, c), local.at[2])

    own_copies = [pltpu.make_async_copy(inputs.at[:, h], toks.at[h, col], local.at[0]) for h in range(2)]
    for copy in own_copies:
        copy.start()

    @pl.loop(0, chunks)
    def _(c):
        for copy in weight_copies(c):
            copy.start()

    @pl.loop(0, units)
    def _(u):
        cot_copy(u).start()

    barrier = pltpu.get_barrier_semaphore()
    for dev in (left_x, right_x, left_y, right_y, left_z, right_z, far_z, sibling):
        pl.semaphore_signal(barrier, inc=1, device_id=dev, device_id_type=pl.DeviceIdType.MESH)
    def all_landed(ref, sem):
        remote(ref, ref, sem, sem, sibling).wait_recv()

    def all_left(ref, sem):
        remote(ref, ref, sem, sem, sibling).wait_send()

    def mask(c):
        pltpu.make_async_copy(weights.at[c], weights.at[c], ws.at[c]).wait()
        for which, pat in enumerate((gate_pat, up_pat)):
            for i in range(weights.shape[1] // BLOCK):
                for j in range(ch // BLOCK):
                    flag = pat[i, c * (ch // BLOCK) + j].astype(F32)
                    rows, cols = pl.ds(i * BLOCK, BLOCK), pl.ds(which * ch + j * BLOCK, BLOCK)
                    weights[c, rows, cols] = (weights[c, rows, cols].astype(F32) * flag).astype(BF16)

    def mask_some(part_of):
        pl.loop(part_of * chunks // 3, (part_of + 1) * chunks // 3)(mask)

    mask_some(0)
    pl.semaphore_wait(barrier, 8)

    mine, from_m, from_p, from_2 = z * 2 + core, zm * 2 + core, zp * 2 + core, z2 * 2 + core
    both = pl.ds(0, 2)

    def spread(h, src, block, k, dev):
        dst = toks.at[h, block]
        return remote(dst if src is None else src, dst, zsent.at[0], zin.at[h, k], dev)

    def own_sends(h):
        devs = (far_z, left_z, right_z, sibling)
        return [spread(h, inputs.at[:, h], mine, k, dev) for k, dev in enumerate(devs)]

    def shares(h):
        return [spread(h, None, block, 4 + k, sibling) for k, block in enumerate((from_2, from_p, from_m))]

    def gather_start(h):
        for copy in own_sends(h):
            copy.start()

    def gather_share(h):
        for k in (1, 2, 0):
            own_sends(h)[k].wait_recv()
            shares(h)[k].start()

    def gather_end(h):
        own_sends(h)[3].wait_recv()
        for copy in shares(h):
            copy.wait_recv()

    gather_start(0)
    acc[...] = jnp.zeros(acc.shape, F32)
    mask_some(1)
    gather_start(1)
    mask_some(2)
    gather_share(0)
    pltpu.make_async_copy(toks.at[both, 0], toks.at[both, 0], local.at[0]).wait()
    pltpu.make_async_copy(cot_v, cot_v, local.at[1]).wait()
    gather_end(0)

    def copies(c, k):
        a, b = pl.ds(0, ch), pl.ds(ch, ch)
        al, ar, bl, br = pl.ds(0, hc), pl.ds(hc, hc), pl.ds(ch, hc), pl.ds(ch + hc, hc)
        first, second, every = pl.ds(0, 2), pl.ds(2, 2), pl.ds(0, 4)
        rows = pl.ds(0, HALF)
        xdev, ydev = (left_x, right_x), (left_y, right_y)
        if k == 0:
            srcs = (part.at[c, 0, first, x2], part.at[c, 0, second, x2], part.at[c, 1, y2, first], part.at[c, 1, y2, second])
            dsts = tuple(half1.at[c, i // 2, i % 2] for i in range(4))
            devs = xdev + ydev
        elif k == 1:
            srcs = (part.at[c, 0, every, xm], part.at[c, 0, every, xp], part.at[c, 1, ym], part.at[c, 1, yp])
            dsts = tuple(full1.at[c, i // 2, i % 2] for i in range(4))
            devs = xdev + ydev
        elif k == 2:
            srcs = (
                sum1.at[c, 0, y2, rows, al], sum1.at[c, 0, y2, rows, ar],
                sum1.at[c, 1, x2, rows, al], sum1.at[c, 1, x2, rows, ar],
            )
            dsts = tuple(half2.at[c, i // 2, i % 2] for i in range(4))
            devs = ydev + xdev
        elif k == 3:
            srcs = (sum1.at[c, 0, ym], sum1.at[c, 0, yp], sum1.at[c, 1, xm], sum1.at[c, 1, xp])
            dsts = tuple(full2.at[c, i // 2, i % 2] for i in range(4))
            devs = ydev + xdev
        elif k == 4:
            ga, gb = grads.at[c, y, x, rows, a], grads.at[c, y, x, rows, b]
            srcs = dsts = (ga, ga, gb, gb)
            devs = ydev + xdev
        elif k == 5:
            srcs = dsts = (
                grads.at[c, yp, x, rows, ar], grads.at[c, ym, x, rows, al],
                grads.at[c, y, xp, rows, br], grads.at[c, y, xm, rows, bl],
            )
            devs = ydev + xdev
        elif k == 6:
            ga, gb = grads.at[c, every, x, rows, a], grads.at[c, y, every, rows, b]
            srcs = dsts = (ga, ga, gb, gb)
            devs = xdev + ydev
        else:
            srcs = dsts = (
                grads.at[c, second, xp, rows, a], grads.at[c, first, xm, rows, a],
                grads.at[c, yp, second, rows, b], grads.at[c, ym, first, rows, b],
            )
            devs = xdev + ydev
        return [
            remote(s, d, send.at[k], recv.at[c, k], dev)
            for s, d, dev in zip(srcs, dsts, devs)
        ]

    def start(c, k):
        for copy in copies(c, k):
            copy.start()

    sizes = (half1, full1, half2, full2, full2, half2, full1, half1)

    def arrived(c, k):
        all_landed(sizes[k].at[c], recv.at[c, k])

    def f(v):
        return v.astype(F32)

    def forward(c):
        product = jnp.dot(
            toks[half_of(c)].reshape(16 * HALF, toks.shape[4]), weights[chunk_of(c)], preferred_element_type=F32
        ).astype(BF16).reshape(4, 4, HALF, 2 * ch)
        part[c, 0] = product[:, :, :, :ch]
        part[c, 1] = product[:, :, :, ch:]
        start(c, 0)

    def merge1(c):
        arrived(c, 0)
        part[c, 0, 0:2, xm] = (f(part[c, 0, 0:2, xm]) + f(half1[c, 0, 0])).astype(BF16)
        part[c, 0, 2:4, xp] = (f(part[c, 0, 2:4, xp]) + f(half1[c, 0, 1])).astype(BF16)
        part[c, 1, ym, 0:2] = (f(part[c, 1, ym, 0:2]) + f(half1[c, 1, 0])).astype(BF16)
        part[c, 1, yp, 2:4] = (f(part[c, 1, yp, 2:4]) + f(half1[c, 1, 1])).astype(BF16)
        start(c, 1)

    def total1(c):
        arrived(c, 1)
        sum1[c, 0] = (f(part[c, 0, :, x]) + f(full1[c, 0, 0]) + f(full1[c, 0, 1])).astype(BF16)
        sum1[c, 1] = (f(part[c, 1, y]) + f(full1[c, 1, 0]) + f(full1[c, 1, 1])).astype(BF16)
        start(c, 2)

    def merge2(c):
        arrived(c, 2)
        for i, (m, p) in enumerate(((ym, yp), (xm, xp))):
            sum1[c, i, m, :, 0:hc] = (f(sum1[c, i, m, :, 0:hc]) + f(half2[c, i, 0])).astype(BF16)
            sum1[c, i, p, :, hc:ch] = (f(sum1[c, i, p, :, hc:ch]) + f(half2[c, i, 1])).astype(BF16)
        start(c, 3)

    def activate(c):
        arrived(c, 3)
        gate_sum = f(sum1[c, 0, y]) + f(full2[c, 0, 0]) + f(full2[c, 0, 1])
        up_sum = f(sum1[c, 1, x]) + f(full2[c, 1, 0]) + f(full2[c, 1, 1])
        sigmoid_gate = jax.nn.sigmoid(gate_sum)
        activated = gate_sum * sigmoid_gate
        cot_f = f(cot_v[c])
        grads[c, y, x, :, 0:ch] = (
            cot_f * up_sum * sigmoid_gate * (1.0 + gate_sum * (1.0 - sigmoid_gate))
        ).astype(BF16)
        grads[c, y, x, :, ch:2 * ch] = (cot_f * activated).astype(BF16)
        start(c, 4)
        hid_v[c] = (activated * up_sum).astype(BF16)
        hid_copy(c).start()

    def forward1(c):
        arrived(c, 4)
        start(c, 5)

    def spread2(c):
        arrived(c, 5)
        start(c, 6)

    def forward2(c):
        arrived(c, 6)
        start(c, 7)

    width = toks.shape[4] // PIECES

    def back(u, n):
        return lax.dot_general(
            grads[u].reshape(16 * HALF, 2 * ch), weights[chunk_of(u), pl.ds(n * width, width), :],
            (((1,), (1,)), ((), ())), preferred_element_type=F32,
        ).reshape(4, 2, 2, HALF, width)

    def backward(u):
        arrived(u, 7)
        for n in range(PIECES):
            acc[n, half_of(u)] += back(u, n)

    stages = (forward, merge1, total1, merge2, activate, forward1, spread2, forward2, backward)
    final = units - 1

    def z_send(src, dst, k, h, n, dev):
        return remote(src, dst, zsent.at[1], zout.at[k, h, n], dev)

    def z_sib(h, n):
        return z_send(zsend.at[h, n], zsib.at[h, n], 0, h, n, sibling)

    def z_full(h, n):
        pairs = ((z2, far_z), (zm, left_z), (zp, right_z))
        return [z_send(zkeep.at[h, n, to], zfull.at[h, n, k], 1, h, n, dev) for k, (to, dev) in enumerate(pairs)]

    def out_copy(h, n):
        return pltpu.make_async_copy(out_v.at[h, n], grad_out.at[:, h, :, pl.ds(n * width, width)], local.at[3])

    def sum_sibling(h, n):
        zsend[h, n] = acc[n, h, :, other].astype(BF16)
        z_sib(h, n).start()

    def sum_last(h, n):
        acc[n, h] += back(final, n)
        sum_sibling(h, n)

    def sum_cores(h, n):
        all_landed(zsib.at[h, n], zout.at[0, h, n])
        total = acc[n, h, :, core] + f(zsib[h, n])
        acc[n, h, :, core] = total
        zkeep[h, n] = total.astype(BF16)
        for copy in z_full(h, n):
            copy.start()

    def sum_end(h, n):
        all_landed(zfull.at[h, n], zout.at[1, h, n])
        terms = acc[n, h, z, core] + f(zfull[h, n, 0]) + f(zfull[h, n, 1]) + f(zfull[h, n, 2])
        out_v[h, n] = terms.astype(BF16)
        out_copy(h, n).start()

    order = (0, 1, 2, 3, 4, 5, 6, 7, 8)
    steps = units + LAGS[8]

    first_done = chunks + LAGS[8]
    events = [(when, lambda g=g: g(1)) for when, g in zip(GATHER_AT, (gather_share, gather_end))]
    for after, piece in zip(SUM_AFTER, (sum_sibling, sum_cores, sum_end)):
        events.append((first_done + after, lambda p=piece: [p(0, n) for n in range(PIECES)]))

    @pl.loop(0, steps - 1)
    def _(step):
        for when, event in events:

            @pl.when(step == when)
            def _():
                event()

        for k in order:
            u = step - LAGS[k]
            last = final if k == 8 else units

            @pl.when((u >= 0) & (u < last))
            def _():
                stages[k](u)

    arrived(final, 7)
    for piece in (sum_last, sum_cores, sum_end):
        for n in range(PIECES):
            piece(1, n)

    for k in range(8):
        all_left(sizes[k], send.at[k])
    for k in range(2):
        all_left(toks.at[both, pl.ds(0, 7)], zsent.at[k])
    pltpu.make_async_copy(hid_v, hid_v, local.at[2]).wait()
    pltpu.make_async_copy(out_v, out_v, local.at[3]).wait()


def hand_over(hidden, grad, hidden_out, grad_out):
    hidden_out[...] = hidden[...]
    grad_out[...] = grad[...]


def shards(inputs, gate_weight, up_weight, gate_pattern, up_pattern, cotangent):
    tokens, depth = inputs.shape
    hidden = gate_weight.shape[1]
    chunks = hidden // CHUNK
    units = 2 * chunks
    ch = CHUNK
    width = depth // PIECES
    any_spec = pl.BlockSpec(memory_space=pl.ANY)
    smem = pl.BlockSpec(memory_space=pltpu.SMEM)
    dma = pltpu.SemaphoreType.DMA
    scratch = [
        pltpu.VMEM((2, 8, 2, HALF, depth), BF16),
        pltpu.VMEM((chunks, depth, 2 * ch), BF16),
        pltpu.VMEM((units, 2, 4, 4, HALF, ch), BF16),
        pltpu.VMEM((units, 2, 2, 2, HALF, ch), BF16),
        pltpu.VMEM((units, 2, 2, 4, HALF, ch), BF16),
        pltpu.VMEM((units, 2, 4, HALF, ch), BF16),
        pltpu.VMEM((units, 2, 2, HALF, ch // 2), BF16),
        pltpu.VMEM((units, 2, 2, HALF, ch), BF16),
        pltpu.VMEM((units, 4, 4, HALF, 2 * ch), BF16),
        pltpu.VMEM((PIECES, 2, 4, 2, 2, HALF, width), F32),
        pltpu.VMEM((2, PIECES, 4, 2, HALF, width), BF16),
        pltpu.VMEM((2, PIECES, 4, 2, HALF, width), BF16),
        pltpu.VMEM((2, PIECES, 4, 2, HALF, width), BF16),
        pltpu.VMEM((2, PIECES, 3, 2, HALF, width), BF16),
        pltpu.VMEM((units, HALF, ch), BF16),
        pltpu.VMEM((units, HALF, ch), BF16),
        pltpu.VMEM((2, PIECES, 2, HALF, width), BF16),
        dma((8,)),
        dma((units, 8)),
        dma((2,)),
        dma((2, 7)),
        dma((2, 2, PIECES)),
        dma((chunks,)),
        dma((4,)),
    ]
    results = pl.pallas_call(
        functools.partial(kernel, chunks),
        out_shape=(
            jax.ShapeDtypeStruct((32, hidden), BF16),
            jax.ShapeDtypeStruct((2, 2, HALF, depth), BF16),
        ),
        in_specs=[any_spec, any_spec, any_spec, smem, smem, any_spec],
        out_specs=(any_spec, any_spec),
        scratch_shapes=scratch,
        compiler_params=pltpu.CompilerParams(
            collective_id=0, has_side_effects=True, vmem_limit_bytes=58 * 1024 * 1024
        ),
        cost_estimate=pl.CostEstimate(
            flops=4 * 512 * depth * 2 * hidden, bytes_accessed=4 * depth * hidden, transcendentals=32 * hidden
        ),
    )(inputs.reshape(2, 2, HALF, depth), gate_weight, up_weight, gate_pattern, up_pattern, cotangent)
    results = (results[0], results[1].reshape(tokens, depth))
    return pl.pallas_call(
        hand_over,
        out_shape=tuple(jax.ShapeDtypeStruct(r.shape, r.dtype) for r in results),
        in_specs=[pl.BlockSpec(memory_space=pltpu.VMEM)] * 2,
        out_specs=(pl.BlockSpec(memory_space=pltpu.VMEM),) * 2,
    )(*results)


def solution(mesh):
    placed = (
        P("col", "row"),
        P("row", "col"),
        P("row", "col"),
        P("row", "col"),
        P("row", "col"),
        P("row", "col"),
    )
    return jax.shard_map(
        shards,
        mesh=mesh,
        in_specs=placed,
        out_specs=(P("row", "col"), P("col", "row")),
        check_vma=False,
    )
```

```python
import functools

import jax
import jax.numpy as jnp
from jax import lax
from jax.experimental import pallas as pl
from jax.experimental.pallas import tpu as pltpu
from jax.sharding import PartitionSpec as P

BLOCK = 128
SIDE = 4
CHUNK = 256
GATHER_AT = (5, 9)
SUM_AFTER = (0, 2, 9)
HALF = 16
PIECES = 2
LAGS = (0, 5, 10, 15, 20, 25, 30, 35, 40)
F32 = jnp.float32
BF16 = jnp.bfloat16


def kernel(
    chunks, inputs, gate_w, up_w, gate_pat, up_pat, cot, hidden_out, grad_out,
    toks, weights, part, half1, full1, sum1, half2, full2, grads, acc, zsend, zsib, zkeep, zfull,
    cot_v, hid_v, out_v, send, recv, zsent, zin, zout, ws, local,
):
    ch = CHUNK
    hc = ch // 2
    row, col = lax.axis_index("row"), lax.axis_index("col")
    y, x = row // SIDE, row % SIDE
    z, core = col // 2, col % 2
    ym, yp, y2 = (y + 3) % SIDE, (y + 1) % SIDE, (y + 2) % SIDE
    xm, xp, x2 = (x + 3) % SIDE, (x + 1) % SIDE, (x + 2) % SIDE
    zm, zp, z2 = (z + 3) % SIDE, (z + 1) % SIDE, (z + 2) % SIDE
    other = 1 - core

    def at(yy, xx):
        return (yy * SIDE + xx, col)

    def atz(zz, cc):
        return (row, zz * 2 + cc)

    left_x, right_x, left_y, right_y = at(y, xm), at(y, xp), at(ym, x), at(yp, x)
    left_z, right_z, far_z, sibling = atz(zm, core), atz(zp, core), atz(z2, core), atz(z, other)

    def remote(src, dst, s, r, dev):
        return pltpu.make_async_remote_copy(
            src_ref=src, dst_ref=dst, send_sem=s, recv_sem=r,
            device_id=dev, device_id_type=pl.DeviceIdType.MESH,
        )

    def weight_copies(c):
        cols = pl.ds(pl.multiple_of(c * ch, ch), ch)
        return (
            pltpu.make_async_copy(gate_w.at[:, cols], weights.at[c, :, pl.ds(0, ch)], ws.at[c]),
            pltpu.make_async_copy(up_w.at[:, cols], weights.at[c, :, pl.ds(ch, ch)], ws.at[c]),
        )

    units = 2 * chunks

    def half_of(u):
        return lax.div(u, chunks)

    def chunk_of(u):
        return lax.rem(u, chunks)

    def strip(ref, u):
        rows = pl.ds(pl.multiple_of(half_of(u) * HALF, HALF), HALF)
        return ref.at[rows, pl.ds(pl.multiple_of(chunk_of(u) * ch, ch), ch)]

    def cot_copy(c):
        return pltpu.make_async_copy(strip(cot, c), cot_v.at[c], local.at[1])

    def hid_copy(c):
        return pltpu.make_async_copy(hid_v.at[c], strip(hidden_out, c), local.at[2])

    own_copies = [pltpu.make_async_copy(inputs.at[:, h], toks.at[h, col], local.at[0]) for h in range(2)]
    for copy in own_copies:
        copy.start()

    @pl.loop(0, chunks)
    def _(c):
        for copy in weight_copies(c):
            copy.start()

    @pl.loop(0, units)
    def _(u):
        cot_copy(u).start()

    barrier = pltpu.get_barrier_semaphore()
    for dev in (left_x, right_x, left_y, right_y, left_z, right_z, far_z, sibling):
        pl.semaphore_signal(barrier, inc=1, device_id=dev, device_id_type=pl.DeviceIdType.MESH)
    def all_landed(ref, sem):
        remote(ref, ref, sem, sem, sibling).wait_recv()

    def all_left(ref, sem):
        remote(ref, ref, sem, sem, sibling).wait_send()

    def mask(c):
        pltpu.make_async_copy(weights.at[c], weights.at[c], ws.at[c]).wait()
        for which, pat in enumerate((gate_pat, up_pat)):
            for i in range(weights.shape[1] // BLOCK):
                for j in range(ch // BLOCK):
                    flag = pat[i, c * (ch // BLOCK) + j].astype(F32)
                    rows, cols = pl.ds(i * BLOCK, BLOCK), pl.ds(which * ch + j * BLOCK, BLOCK)
                    weights[c, rows, cols] = (weights[c, rows, cols].astype(F32) * flag).astype(BF16)

    def mask_some(part_of):
        pl.loop(part_of * chunks // 3, (part_of + 1) * chunks // 3)(mask)

    mask_some(0)
    pl.semaphore_wait(barrier, 8)

    mine, from_m, from_p, from_2 = z * 2 + core, zm * 2 + core, zp * 2 + core, z2 * 2 + core
    both = pl.ds(0, 2)

    def spread(h, src, block, k, dev):
        dst = toks.at[h, block]
        return remote(dst if src is None else src, dst, zsent.at[0], zin.at[h, k], dev)

    def own_sends(h):
        devs = (far_z, left_z, right_z, sibling)
        return [spread(h, inputs.at[:, h], mine, k, dev) for k, dev in enumerate(devs)]

    def shares(h):
        return [spread(h, None, block, 4 + k, sibling) for k, block in enumerate((from_2, from_p, from_m))]

    def gather_start(h):
        for copy in own_sends(h):
            copy.start()

    def gather_share(h):
        for k in (1, 2, 0):
            own_sends(h)[k].wait_recv()
            shares(h)[k].start()

    def gather_end(h):
        own_sends(h)[3].wait_recv()
        for copy in shares(h):
            copy.wait_recv()

    gather_start(0)
    acc[...] = jnp.zeros(acc.shape, F32)
    mask_some(1)
    gather_start(1)
    mask_some(2)
    gather_share(0)
    pltpu.make_async_copy(toks.at[both, 0], toks.at[both, 0], local.at[0]).wait()
    pltpu.make_async_copy(cot_v, cot_v, local.at[1]).wait()
    gather_end(0)

    def copies(c, k):
        a, b = pl.ds(0, ch), pl.ds(ch, ch)
        al, ar, bl, br = pl.ds(0, hc), pl.ds(hc, hc), pl.ds(ch, hc), pl.ds(ch + hc, hc)
        first, second, every = pl.ds(0, 2), pl.ds(2, 2), pl.ds(0, 4)
        rows = pl.ds(0, HALF)
        xdev, ydev = (left_x, right_x), (left_y, right_y)
        if k == 0:
            srcs = (part.at[c, 0, first, x2], part.at[c, 0, second, x2], part.at[c, 1, y2, first], part.at[c, 1, y2, second])
            dsts = tuple(half1.at[c, i // 2, i % 2] for i in range(4))
            devs = xdev + ydev
        elif k == 1:
            srcs = (part.at[c, 0, every, xm], part.at[c, 0, every, xp], part.at[c, 1, ym], part.at[c, 1, yp])
            dsts = tuple(full1.at[c, i // 2, i % 2] for i in range(4))
            devs = xdev + ydev
        elif k == 2:
            srcs = (
                sum1.at[c, 0, y2, rows, al], sum1.at[c, 0, y2, rows, ar],
                sum1.at[c, 1, x2, rows, al], sum1.at[c, 1, x2, rows, ar],
            )
            dsts = tuple(half2.at[c, i // 2, i % 2] for i in range(4))
            devs = ydev + xdev
        elif k == 3:
            srcs = (sum1.at[c, 0, ym], sum1.at[c, 0, yp], sum1.at[c, 1, xm], sum1.at[c, 1, xp])
            dsts = tuple(full2.at[c, i // 2, i % 2] for i in range(4))
            devs = ydev + xdev
        elif k == 4:
            ga, gb = grads.at[c, y, x, rows, a], grads.at[c, y, x, rows, b]
            srcs = dsts = (ga, ga, gb, gb)
            devs = ydev + xdev
        elif k == 5:
            srcs = dsts = (
                grads.at[c, yp, x, rows, ar], grads.at[c, ym, x, rows, al],
                grads.at[c, y, xp, rows, br], grads.at[c, y, xm, rows, bl],
            )
            devs = ydev + xdev
        elif k == 6:
            ga, gb = grads.at[c, every, x, rows, a], grads.at[c, y, every, rows, b]
            srcs = dsts = (ga, ga, gb, gb)
            devs = xdev + ydev
        else:
            srcs = dsts = (
                grads.at[c, second, xp, rows, a], grads.at[c, first, xm, rows, a],
                grads.at[c, yp, second, rows, b], grads.at[c, ym, first, rows, b],
            )
            devs = xdev + ydev
        return [
            remote(s, d, send.at[k], recv.at[chunk_of(c), k], dev)
            for s, d, dev in zip(srcs, dsts, devs)
        ]

    def start(c, k):
        for copy in copies(c, k):
            copy.start()

    sizes = (half1, full1, half2, full2, full2, half2, full1, half1)

    def arrived(c, k):
        all_landed(sizes[k].at[c], recv.at[chunk_of(c), k])

    def f(v):
        return v.astype(F32)

    def forward(c):
        product = jnp.dot(
            toks[half_of(c)].reshape(16 * HALF, toks.shape[4]), weights[chunk_of(c)], preferred_element_type=F32
        ).astype(BF16).reshape(4, 4, HALF, 2 * ch)
        part[c, 0] = product[:, :, :, :ch]
        part[c, 1] = product[:, :, :, ch:]
        start(c, 0)

    def merge1(c):
        arrived(c, 0)
        part[c, 0, 0:2, xm] = (f(part[c, 0, 0:2, xm]) + f(half1[c, 0, 0])).astype(BF16)
        part[c, 0, 2:4, xp] = (f(part[c, 0, 2:4, xp]) + f(half1[c, 0, 1])).astype(BF16)
        part[c, 1, ym, 0:2] = (f(part[c, 1, ym, 0:2]) + f(half1[c, 1, 0])).astype(BF16)
        part[c, 1, yp, 2:4] = (f(part[c, 1, yp, 2:4]) + f(half1[c, 1, 1])).astype(BF16)
        start(c, 1)

    def total1(c):
        arrived(c, 1)
        sum1[c, 0] = (f(part[c, 0, :, x]) + f(full1[c, 0, 0]) + f(full1[c, 0, 1])).astype(BF16)
        sum1[c, 1] = (f(part[c, 1, y]) + f(full1[c, 1, 0]) + f(full1[c, 1, 1])).astype(BF16)
        start(c, 2)

    def merge2(c):
        arrived(c, 2)
        for i, (m, p) in enumerate(((ym, yp), (xm, xp))):
            sum1[c, i, m, :, 0:hc] = (f(sum1[c, i, m, :, 0:hc]) + f(half2[c, i, 0])).astype(BF16)
            sum1[c, i, p, :, hc:ch] = (f(sum1[c, i, p, :, hc:ch]) + f(half2[c, i, 1])).astype(BF16)
        start(c, 3)

    def activate(c):
        arrived(c, 3)
        gate_sum = f(sum1[c, 0, y]) + f(full2[c, 0, 0]) + f(full2[c, 0, 1])
        up_sum = f(sum1[c, 1, x]) + f(full2[c, 1, 0]) + f(full2[c, 1, 1])
        sigmoid_gate = jax.nn.sigmoid(gate_sum)
        activated = gate_sum * sigmoid_gate
        cot_f = f(cot_v[c])
        grads[c, y, x, :, 0:ch] = (
            cot_f * up_sum * sigmoid_gate * (1.0 + gate_sum * (1.0 - sigmoid_gate))
        ).astype(BF16)
        grads[c, y, x, :, ch:2 * ch] = (cot_f * activated).astype(BF16)
        start(c, 4)
        hid_v[c] = (activated * up_sum).astype(BF16)
        hid_copy(c).start()

    def forward1(c):
        arrived(c, 4)
        start(c, 5)

    def spread2(c):
        arrived(c, 5)
        start(c, 6)

    def forward2(c):
        arrived(c, 6)
        start(c, 7)

    width = toks.shape[4] // PIECES

    def back(u, n):
        return lax.dot_general(
            grads[u].reshape(16 * HALF, 2 * ch), weights[chunk_of(u), pl.ds(n * width, width), :],
            (((1,), (1,)), ((), ())), preferred_element_type=F32,
        ).reshape(4, 2, 2, HALF, width)

    def backward(u):
        arrived(u, 7)
        for n in range(PIECES):
            acc[n, half_of(u)] += back(u, n)

    stages = (forward, merge1, total1, merge2, activate, forward1, spread2, forward2, backward)
    final = units - 1

    def z_send(src, dst, k, h, n, dev):
        return remote(src, dst, zsent.at[1], zout.at[k, h, n], dev)

    def z_sib(h, n):
        return z_send(zsend.at[h, n], zsib.at[h, n], 0, h, n, sibling)

    def z_full(h, n):
        pairs = ((z2, far_z), (zm, left_z), (zp, right_z))
        return [z_send(zkeep.at[h, n, to], zfull.at[h, n, k], 1, h, n, dev) for k, (to, dev) in enumerate(pairs)]

    def out_copy(h, n):
        return pltpu.make_async_copy(out_v.at[h, n], grad_out.at[:, h, :, pl.ds(n * width, width)], local.at[3])

    def sum_sibling(h, n):
        zsend[h, n] = acc[n, h, :, other].astype(BF16)
        z_sib(h, n).start()

    def sum_last(h, n):
        acc[n, h] += back(final, n)
        sum_sibling(h, n)

    def sum_cores(h, n):
        all_landed(zsib.at[h, n], zout.at[0, h, n])
        total = acc[n, h, :, core] + f(zsib[h, n])
        acc[n, h, :, core] = total
        zkeep[h, n] = total.astype(BF16)
        for copy in z_full(h, n):
            copy.start()

    def sum_end(h, n):
        all_landed(zfull.at[h, n], zout.at[1, h, n])
        terms = acc[n, h, z, core] + f(zfull[h, n, 0]) + f(zfull[h, n, 1]) + f(zfull[h, n, 2])
        out_v[h, n] = terms.astype(BF16)
        out_copy(h, n).start()

    order = (0, 1, 2, 3, 4, 5, 6, 7, 8)
    steps = units + LAGS[8]

    first_done = chunks + LAGS[8]
    events = [(when, lambda g=g: g(1)) for when, g in zip(GATHER_AT, (gather_share, gather_end))]
    for after, piece in zip(SUM_AFTER, (sum_sibling, sum_cores, sum_end)):
        events.append((first_done + after, lambda p=piece: [p(0, n) for n in range(PIECES)]))

    @pl.loop(0, steps - 1)
    def _(step):
        for when, event in events:

            @pl.when(step == when)
            def _():
                event()

        for k in order:
            u = step - LAGS[k]
            last = final if k == 8 else units

            @pl.when((u >= 0) & (u < last))
            def _():
                stages[k](u)

    arrived(final, 7)
    for piece in (sum_last, sum_cores, sum_end):
        for n in range(PIECES):
            piece(1, n)

    for k in range(8):
        all_left(sizes[k], send.at[k])
    for k in range(2):
        all_left(toks.at[both, pl.ds(0, 7)], zsent.at[k])
    pltpu.make_async_copy(hid_v, hid_v, local.at[2]).wait()
    pltpu.make_async_copy(out_v, out_v, local.at[3]).wait()


def hand_over(hidden, grad, hidden_out, grad_out):
    hidden_out[...] = hidden[...]
    grad_out[...] = grad[...]


def shards(inputs, gate_weight, up_weight, gate_pattern, up_pattern, cotangent):
    tokens, depth = inputs.shape
    hidden = gate_weight.shape[1]
    chunks = hidden // CHUNK
    units = 2 * chunks
    ch = CHUNK
    width = depth // PIECES
    any_spec = pl.BlockSpec(memory_space=pl.ANY)
    smem = pl.BlockSpec(memory_space=pltpu.SMEM)
    dma = pltpu.SemaphoreType.DMA
    scratch = [
        pltpu.VMEM((2, 8, 2, HALF, depth), BF16),
        pltpu.VMEM((chunks, depth, 2 * ch), BF16),
        pltpu.VMEM((units, 2, 4, 4, HALF, ch), BF16),
        pltpu.VMEM((units, 2, 2, 2, HALF, ch), BF16),
        pltpu.VMEM((units, 2, 2, 4, HALF, ch), BF16),
        pltpu.VMEM((units, 2, 4, HALF, ch), BF16),
        pltpu.VMEM((units, 2, 2, HALF, ch // 2), BF16),
        pltpu.VMEM((units, 2, 2, HALF, ch), BF16),
        pltpu.VMEM((units, 4, 4, HALF, 2 * ch), BF16),
        pltpu.VMEM((PIECES, 2, 4, 2, 2, HALF, width), F32),
        pltpu.VMEM((2, PIECES, 4, 2, HALF, width), BF16),
        pltpu.VMEM((2, PIECES, 4, 2, HALF, width), BF16),
        pltpu.VMEM((2, PIECES, 4, 2, HALF, width), BF16),
        pltpu.VMEM((2, PIECES, 3, 2, HALF, width), BF16),
        pltpu.VMEM((units, HALF, ch), BF16),
        pltpu.VMEM((units, HALF, ch), BF16),
        pltpu.VMEM((2, PIECES, 2, HALF, width), BF16),
        dma((8,)),
        dma((chunks, 8)),
        dma((2,)),
        dma((2, 7)),
        dma((2, 2, PIECES)),
        dma((chunks,)),
        dma((4,)),
    ]
    results = pl.pallas_call(
        functools.partial(kernel, chunks),
        out_shape=(
            jax.ShapeDtypeStruct((32, hidden), BF16),
            jax.ShapeDtypeStruct((2, 2, HALF, depth), BF16),
        ),
        in_specs=[any_spec, any_spec, any_spec, smem, smem, any_spec],
        out_specs=(any_spec, any_spec),
        scratch_shapes=scratch,
        compiler_params=pltpu.CompilerParams(
            collective_id=0, has_side_effects=True, vmem_limit_bytes=58 * 1024 * 1024
        ),
        cost_estimate=pl.CostEstimate(
            flops=4 * 512 * depth * 2 * hidden, bytes_accessed=4 * depth * hidden, transcendentals=32 * hidden
        ),
    )(inputs.reshape(2, 2, HALF, depth), gate_weight, up_weight, gate_pattern, up_pattern, cotangent)
    results = (results[0], results[1].reshape(tokens, depth))
    return pl.pallas_call(
        hand_over,
        out_shape=tuple(jax.ShapeDtypeStruct(r.shape, r.dtype) for r in results),
        in_specs=[pl.BlockSpec(memory_space=pltpu.VMEM)] * 2,
        out_specs=(pl.BlockSpec(memory_space=pltpu.VMEM),) * 2,
    )(*results)


def solution(mesh):
    placed = (
        P("col", "row"),
        P("row", "col"),
        P("row", "col"),
        P("row", "col"),
        P("row", "col"),
        P("row", "col"),
    )
    return jax.shard_map(
        shards,
        mesh=mesh,
        in_specs=placed,
        out_specs=(P("row", "col"), P("col", "row")),
        check_vma=False,
    )
```

```python
import functools

import jax
import jax.numpy as jnp
from jax import lax
from jax.experimental import pallas as pl
from jax.experimental.pallas import tpu as pltpu
from jax.sharding import PartitionSpec as P

BLOCK = 128
SIDE = 4
CHUNK = 256
GATHER_AT = (5, 9)
SUM_AFTER = (0, 2, 9)
HALF = 16
PIECES = 2
LAGS = (0, 5, 10, 15, 20, 25, 30, 35, 40)
F32 = jnp.float32
BF16 = jnp.bfloat16


def kernel(
    chunks, inputs, gate_w, up_w, gate_pat, up_pat, cot, hidden_out, grad_out,
    toks, weights, part, half1, full1, sum1, half2, full2, grads, acc, zsend, zsib, zkeep, zfull,
    cot_v, hid_v, out_v, send, recv, zsent, zin, zout, ws, local,
):
    ch = CHUNK
    hc = ch // 2
    row, col = lax.axis_index("row"), lax.axis_index("col")
    y, x = row // SIDE, row % SIDE
    z, core = col // 2, col % 2
    ym, yp, y2 = (y + 3) % SIDE, (y + 1) % SIDE, (y + 2) % SIDE
    xm, xp, x2 = (x + 3) % SIDE, (x + 1) % SIDE, (x + 2) % SIDE
    zm, zp, z2 = (z + 3) % SIDE, (z + 1) % SIDE, (z + 2) % SIDE
    other = 1 - core

    def at(yy, xx):
        return (yy * SIDE + xx, col)

    def atz(zz, cc):
        return (row, zz * 2 + cc)

    left_x, right_x, left_y, right_y = at(y, xm), at(y, xp), at(ym, x), at(yp, x)
    left_z, right_z, far_z, sibling = atz(zm, core), atz(zp, core), atz(z2, core), atz(z, other)

    def remote(src, dst, s, r, dev):
        return pltpu.make_async_remote_copy(
            src_ref=src, dst_ref=dst, send_sem=s, recv_sem=r,
            device_id=dev, device_id_type=pl.DeviceIdType.MESH,
        )

    def weight_copies(c):
        cols = pl.ds(pl.multiple_of(c * ch, ch), ch)
        return (
            pltpu.make_async_copy(gate_w.at[:, cols], weights.at[c, :, pl.ds(0, ch)], ws.at[c]),
            pltpu.make_async_copy(up_w.at[:, cols], weights.at[c, :, pl.ds(ch, ch)], ws.at[c]),
        )

    units = 2 * chunks

    def half_of(u):
        return lax.div(u, chunks)

    def chunk_of(u):
        return lax.rem(u, chunks)

    def strip(ref, u):
        rows = pl.ds(pl.multiple_of(half_of(u) * HALF, HALF), HALF)
        return ref.at[rows, pl.ds(pl.multiple_of(chunk_of(u) * ch, ch), ch)]

    def cot_copy(c):
        return pltpu.make_async_copy(strip(cot, c), cot_v.at[c], local.at[1])

    def hid_copy(c):
        return pltpu.make_async_copy(hid_v.at[c], strip(hidden_out, c), local.at[2])

    own_copies = [pltpu.make_async_copy(inputs.at[:, h], toks.at[h, col], local.at[0]) for h in range(2)]
    for copy in own_copies:
        copy.start()

    @pl.loop(0, chunks)
    def _(c):
        for copy in weight_copies(c):
            copy.start()

    @pl.loop(0, units)
    def _(u):
        cot_copy(u).start()

    barrier = pltpu.get_barrier_semaphore()
    for dev in (left_x, right_x, left_y, right_y, left_z, right_z, far_z, sibling):
        pl.semaphore_signal(barrier, inc=1, device_id=dev, device_id_type=pl.DeviceIdType.MESH)
    def all_landed(ref, sem):
        remote(ref, ref, sem, sem, sibling).wait_recv()

    def all_left(ref, sem):
        remote(ref, ref, sem, sem, sibling).wait_send()

    def mask(c):
        pltpu.make_async_copy(weights.at[c], weights.at[c], ws.at[c]).wait()
        for which, pat in enumerate((gate_pat, up_pat)):
            for i in range(weights.shape[1] // BLOCK):
                for j in range(ch // BLOCK):
                    flag = pat[i, c * (ch // BLOCK) + j].astype(F32)
                    rows, cols = pl.ds(i * BLOCK, BLOCK), pl.ds(which * ch + j * BLOCK, BLOCK)
                    weights[c, rows, cols] = (weights[c, rows, cols].astype(F32) * flag).astype(BF16)

    def mask_some(part_of):
        pl.loop(part_of * chunks // 3, (part_of + 1) * chunks // 3)(mask)

    mask_some(0)
    pl.semaphore_wait(barrier, 8)

    mine, from_m, from_p, from_2 = z * 2 + core, zm * 2 + core, zp * 2 + core, z2 * 2 + core
    both = pl.ds(0, 2)

    def spread(h, src, block, k, dev):
        dst = toks.at[h, block]
        return remote(dst if src is None else src, dst, zsent.at[0], zin.at[h, k], dev)

    def own_sends(h):
        devs = (far_z, left_z, right_z, sibling)
        return [spread(h, inputs.at[:, h], mine, k, dev) for k, dev in enumerate(devs)]

    def shares(h):
        return [spread(h, None, block, 4 + k, sibling) for k, block in enumerate((from_2, from_p, from_m))]

    def gather_start(h):
        for copy in own_sends(h):
            copy.start()

    def gather_share(h):
        for k in (1, 2, 0):
            own_sends(h)[k].wait_recv()
            shares(h)[k].start()

    def gather_end(h):
        own_sends(h)[3].wait_recv()
        for copy in shares(h):
            copy.wait_recv()

    gather_start(0)
    acc[...] = jnp.zeros(acc.shape, F32)
    mask_some(1)
    gather_start(1)
    gather_share(0)
    pltpu.make_async_copy(toks.at[both, 0], toks.at[both, 0], local.at[0]).wait()
    pltpu.make_async_copy(cot_v, cot_v, local.at[1]).wait()
    gather_end(0)

    def copies(c, k):
        a, b = pl.ds(0, ch), pl.ds(ch, ch)
        al, ar, bl, br = pl.ds(0, hc), pl.ds(hc, hc), pl.ds(ch, hc), pl.ds(ch + hc, hc)
        first, second, every = pl.ds(0, 2), pl.ds(2, 2), pl.ds(0, 4)
        rows = pl.ds(0, HALF)
        xdev, ydev = (left_x, right_x), (left_y, right_y)
        if k == 0:
            srcs = (part.at[c, 0, first, x2], part.at[c, 0, second, x2], part.at[c, 1, y2, first], part.at[c, 1, y2, second])
            dsts = tuple(half1.at[c, i // 2, i % 2] for i in range(4))
            devs = xdev + ydev
        elif k == 1:
            srcs = (part.at[c, 0, every, xm], part.at[c, 0, every, xp], part.at[c, 1, ym], part.at[c, 1, yp])
            dsts = tuple(full1.at[c, i // 2, i % 2] for i in range(4))
            devs = xdev + ydev
        elif k == 2:
            srcs = (
                sum1.at[c, 0, y2, rows, al], sum1.at[c, 0, y2, rows, ar],
                sum1.at[c, 1, x2, rows, al], sum1.at[c, 1, x2, rows, ar],
            )
            dsts = tuple(half2.at[c, i // 2, i % 2] for i in range(4))
            devs = ydev + xdev
        elif k == 3:
            srcs = (sum1.at[c, 0, ym], sum1.at[c, 0, yp], sum1.at[c, 1, xm], sum1.at[c, 1, xp])
            dsts = tuple(full2.at[c, i // 2, i % 2] for i in range(4))
            devs = ydev + xdev
        elif k == 4:
            ga, gb = grads.at[c, y, x, rows, a], grads.at[c, y, x, rows, b]
            srcs = dsts = (ga, ga, gb, gb)
            devs = ydev + xdev
        elif k == 5:
            srcs = dsts = (
                grads.at[c, yp, x, rows, ar], grads.at[c, ym, x, rows, al],
                grads.at[c, y, xp, rows, br], grads.at[c, y, xm, rows, bl],
            )
            devs = ydev + xdev
        elif k == 6:
            ga, gb = grads.at[c, every, x, rows, a], grads.at[c, y, every, rows, b]
            srcs = dsts = (ga, ga, gb, gb)
            devs = xdev + ydev
        else:
            srcs = dsts = (
                grads.at[c, second, xp, rows, a], grads.at[c, first, xm, rows, a],
                grads.at[c, yp, second, rows, b], grads.at[c, ym, first, rows, b],
            )
            devs = xdev + ydev
        return [
            remote(s, d, send.at[k], recv.at[chunk_of(c), k], dev)
            for s, d, dev in zip(srcs, dsts, devs)
        ]

    def start(c, k):
        for copy in copies(c, k):
            copy.start()

    sizes = (half1, full1, half2, full2, full2, half2, full1, half1)

    def arrived(c, k):
        all_landed(sizes[k].at[c], recv.at[chunk_of(c), k])

    def f(v):
        return v.astype(F32)

    def forward(c):
        product = jnp.dot(
            toks[half_of(c)].reshape(16 * HALF, toks.shape[4]), weights[chunk_of(c)], preferred_element_type=F32
        ).astype(BF16).reshape(4, 4, HALF, 2 * ch)
        part[c, 0] = product[:, :, :, :ch]
        part[c, 1] = product[:, :, :, ch:]
        start(c, 0)

    def merge1(c):
        arrived(c, 0)
        part[c, 0, 0:2, xm] = (f(part[c, 0, 0:2, xm]) + f(half1[c, 0, 0])).astype(BF16)
        part[c, 0, 2:4, xp] = (f(part[c, 0, 2:4, xp]) + f(half1[c, 0, 1])).astype(BF16)
        part[c, 1, ym, 0:2] = (f(part[c, 1, ym, 0:2]) + f(half1[c, 1, 0])).astype(BF16)
        part[c, 1, yp, 2:4] = (f(part[c, 1, yp, 2:4]) + f(half1[c, 1, 1])).astype(BF16)
        start(c, 1)

    def total1(c):
        arrived(c, 1)
        sum1[c, 0] = (f(part[c, 0, :, x]) + f(full1[c, 0, 0]) + f(full1[c, 0, 1])).astype(BF16)
        sum1[c, 1] = (f(part[c, 1, y]) + f(full1[c, 1, 0]) + f(full1[c, 1, 1])).astype(BF16)
        start(c, 2)

    def merge2(c):
        arrived(c, 2)
        for i, (m, p) in enumerate(((ym, yp), (xm, xp))):
            sum1[c, i, m, :, 0:hc] = (f(sum1[c, i, m, :, 0:hc]) + f(half2[c, i, 0])).astype(BF16)
            sum1[c, i, p, :, hc:ch] = (f(sum1[c, i, p, :, hc:ch]) + f(half2[c, i, 1])).astype(BF16)
        start(c, 3)

    def activate(c):
        arrived(c, 3)
        gate_sum = f(sum1[c, 0, y]) + f(full2[c, 0, 0]) + f(full2[c, 0, 1])
        up_sum = f(sum1[c, 1, x]) + f(full2[c, 1, 0]) + f(full2[c, 1, 1])
        sigmoid_gate = jax.nn.sigmoid(gate_sum)
        activated = gate_sum * sigmoid_gate
        cot_f = f(cot_v[c])
        grads[c, y, x, :, 0:ch] = (
            cot_f * up_sum * sigmoid_gate * (1.0 + gate_sum * (1.0 - sigmoid_gate))
        ).astype(BF16)
        grads[c, y, x, :, ch:2 * ch] = (cot_f * activated).astype(BF16)
        start(c, 4)
        hid_v[c] = (activated * up_sum).astype(BF16)
        hid_copy(c).start()

    def forward1(c):
        arrived(c, 4)
        start(c, 5)

    def spread2(c):
        arrived(c, 5)
        start(c, 6)

    def forward2(c):
        arrived(c, 6)
        start(c, 7)

    width = toks.shape[4] // PIECES

    def back(u, n):
        return lax.dot_general(
            grads[u].reshape(16 * HALF, 2 * ch), weights[chunk_of(u), pl.ds(n * width, width), :],
            (((1,), (1,)), ((), ())), preferred_element_type=F32,
        ).reshape(4, 2, 2, HALF, width)

    def backward(u):
        arrived(u, 7)
        for n in range(PIECES):
            acc[n, half_of(u)] += back(u, n)

    stages = (forward, merge1, total1, merge2, activate, forward1, spread2, forward2, backward)
    final = units - 1

    def z_send(src, dst, k, h, n, dev):
        return remote(src, dst, zsent.at[1], zout.at[k, h, n], dev)

    def z_sib(h, n):
        return z_send(zsend.at[h, n], zsib.at[h, n], 0, h, n, sibling)

    def z_full(h, n):
        pairs = ((z2, far_z), (zm, left_z), (zp, right_z))
        return [z_send(zkeep.at[h, n, to], zfull.at[h, n, k], 1, h, n, dev) for k, (to, dev) in enumerate(pairs)]

    def out_copy(h, n):
        return pltpu.make_async_copy(out_v.at[h, n], grad_out.at[:, h, :, pl.ds(n * width, width)], local.at[3])

    def sum_sibling(h, n):
        zsend[h, n] = acc[n, h, :, other].astype(BF16)
        z_sib(h, n).start()

    def sum_last(h, n):
        acc[n, h] += back(final, n)
        sum_sibling(h, n)

    def sum_cores(h, n):
        all_landed(zsib.at[h, n], zout.at[0, h, n])
        total = acc[n, h, :, core] + f(zsib[h, n])
        acc[n, h, :, core] = total
        zkeep[h, n] = total.astype(BF16)
        for copy in z_full(h, n):
            copy.start()

    def sum_end(h, n):
        all_landed(zfull.at[h, n], zout.at[1, h, n])
        terms = acc[n, h, z, core] + f(zfull[h, n, 0]) + f(zfull[h, n, 1]) + f(zfull[h, n, 2])
        out_v[h, n] = terms.astype(BF16)
        out_copy(h, n).start()

    order = (0, 1, 2, 3, 4, 5, 6, 7, 8)
    steps = units + LAGS[8]

    first_done = chunks + LAGS[8]
    events = [(when, lambda g=g: g(1)) for when, g in zip(GATHER_AT, (gather_share, gather_end))]
    for after, piece in zip(SUM_AFTER, (sum_sibling, sum_cores, sum_end)):
        events.append((first_done + after, lambda p=piece: [p(0, n) for n in range(PIECES)]))

    @pl.loop(0, steps - 1)
    def _(step):
        @pl.when((step >= 2 * chunks // 3) & (step < chunks))
        def _():
            mask(step)

        for when, event in events:

            @pl.when(step == when)
            def _():
                event()

        for k in order:
            u = step - LAGS[k]
            last = final if k == 8 else units

            @pl.when((u >= 0) & (u < last))
            def _():
                stages[k](u)

    arrived(final, 7)
    for piece in (sum_last, sum_cores, sum_end):
        for n in range(PIECES):
            piece(1, n)

    for k in range(8):
        all_left(sizes[k], send.at[k])
    for k in range(2):
        all_left(toks.at[both, pl.ds(0, 7)], zsent.at[k])
    pltpu.make_async_copy(hid_v, hid_v, local.at[2]).wait()
    pltpu.make_async_copy(out_v, out_v, local.at[3]).wait()


def hand_over(hidden, grad, hidden_out, grad_out):
    hidden_out[...] = hidden[...]
    grad_out[...] = grad[...]


def shards(inputs, gate_weight, up_weight, gate_pattern, up_pattern, cotangent):
    tokens, depth = inputs.shape
    hidden = gate_weight.shape[1]
    chunks = hidden // CHUNK
    units = 2 * chunks
    ch = CHUNK
    width = depth // PIECES
    any_spec = pl.BlockSpec(memory_space=pl.ANY)
    smem = pl.BlockSpec(memory_space=pltpu.SMEM)
    dma = pltpu.SemaphoreType.DMA
    scratch = [
        pltpu.VMEM((2, 8, 2, HALF, depth), BF16),
        pltpu.VMEM((chunks, depth, 2 * ch), BF16),
        pltpu.VMEM((units, 2, 4, 4, HALF, ch), BF16),
        pltpu.VMEM((units, 2, 2, 2, HALF, ch), BF16),
        pltpu.VMEM((units, 2, 2, 4, HALF, ch), BF16),
        pltpu.VMEM((units, 2, 4, HALF, ch), BF16),
        pltpu.VMEM((units, 2, 2, HALF, ch // 2), BF16),
        pltpu.VMEM((units, 2, 2, HALF, ch), BF16),
        pltpu.VMEM((units, 4, 4, HALF, 2 * ch), BF16),
        pltpu.VMEM((PIECES, 2, 4, 2, 2, HALF, width), F32),
        pltpu.VMEM((2, PIECES, 4, 2, HALF, width), BF16),
        pltpu.VMEM((2, PIECES, 4, 2, HALF, width), BF16),
        pltpu.VMEM((2, PIECES, 4, 2, HALF, width), BF16),
        pltpu.VMEM((2, PIECES, 3, 2, HALF, width), BF16),
        pltpu.VMEM((units, HALF, ch), BF16),
        pltpu.VMEM((units, HALF, ch), BF16),
        pltpu.VMEM((2, PIECES, 2, HALF, width), BF16),
        dma((8,)),
        dma((chunks, 8)),
        dma((2,)),
        dma((2, 7)),
        dma((2, 2, PIECES)),
        dma((chunks,)),
        dma((4,)),
    ]
    results = pl.pallas_call(
        functools.partial(kernel, chunks),
        out_shape=(
            jax.ShapeDtypeStruct((32, hidden), BF16),
            jax.ShapeDtypeStruct((2, 2, HALF, depth), BF16),
        ),
        in_specs=[any_spec, any_spec, any_spec, smem, smem, any_spec],
        out_specs=(any_spec, any_spec),
        scratch_shapes=scratch,
        compiler_params=pltpu.CompilerParams(
            collective_id=0, has_side_effects=True, vmem_limit_bytes=58 * 1024 * 1024
        ),
        cost_estimate=pl.CostEstimate(
            flops=4 * 512 * depth * 2 * hidden, bytes_accessed=4 * depth * hidden, transcendentals=32 * hidden
        ),
    )(inputs.reshape(2, 2, HALF, depth), gate_weight, up_weight, gate_pattern, up_pattern, cotangent)
    results = (results[0], results[1].reshape(tokens, depth))
    return pl.pallas_call(
        hand_over,
        out_shape=tuple(jax.ShapeDtypeStruct(r.shape, r.dtype) for r in results),
        in_specs=[pl.BlockSpec(memory_space=pltpu.VMEM)] * 2,
        out_specs=(pl.BlockSpec(memory_space=pltpu.VMEM),) * 2,
    )(*results)


def solution(mesh):
    placed = (
        P("col", "row"),
        P("row", "col"),
        P("row", "col"),
        P("row", "col"),
        P("row", "col"),
        P("row", "col"),
    )
    return jax.shard_map(
        shards,
        mesh=mesh,
        in_specs=placed,
        out_specs=(P("row", "col"), P("col", "row")),
        check_vma=False,
    )
```

```python
import functools

import jax
import jax.numpy as jnp
from jax import lax
from jax.experimental import pallas as pl
from jax.experimental.pallas import tpu as pltpu
from jax.sharding import PartitionSpec as P

BLOCK = 128
SIDE = 4
CHUNK = 256
GATHER_AT = (5, 9)
SUM_AFTER = (0, 2, 9)
HALF = 16
PIECES = 2
LAGS = (0, 5, 10, 15, 20, 25, 30, 35, 40)
F32 = jnp.float32
BF16 = jnp.bfloat16


def kernel(
    chunks, inputs, gate_w, up_w, gate_pat, up_pat, cot, hidden_out, grad_out,
    toks, weights, part, half1, full1, sum1, half2, full2, grads, acc, zsend, zsib, zkeep, zfull,
    cot_v, hid_v, out_v, send, recv, zsent, zin, zout, ws, local,
):
    ch = CHUNK
    hc = ch // 2
    row, col = lax.axis_index("row"), lax.axis_index("col")
    y, x = row // SIDE, row % SIDE
    z, core = col // 2, col % 2
    ym, yp, y2 = (y + 3) % SIDE, (y + 1) % SIDE, (y + 2) % SIDE
    xm, xp, x2 = (x + 3) % SIDE, (x + 1) % SIDE, (x + 2) % SIDE
    zm, zp, z2 = (z + 3) % SIDE, (z + 1) % SIDE, (z + 2) % SIDE
    other = 1 - core

    def at(yy, xx):
        return (yy * SIDE + xx, col)

    def atz(zz, cc):
        return (row, zz * 2 + cc)

    left_x, right_x, left_y, right_y = at(y, xm), at(y, xp), at(ym, x), at(yp, x)
    left_z, right_z, far_z, sibling = atz(zm, core), atz(zp, core), atz(z2, core), atz(z, other)

    def remote(src, dst, s, r, dev):
        return pltpu.make_async_remote_copy(
            src_ref=src, dst_ref=dst, send_sem=s, recv_sem=r,
            device_id=dev, device_id_type=pl.DeviceIdType.MESH,
        )

    def weight_copies(c):
        cols = pl.ds(pl.multiple_of(c * ch, ch), ch)
        return (
            pltpu.make_async_copy(gate_w.at[:, cols], weights.at[c, :, pl.ds(0, ch)], ws.at[c]),
            pltpu.make_async_copy(up_w.at[:, cols], weights.at[c, :, pl.ds(ch, ch)], ws.at[c]),
        )

    units = 2 * chunks

    def half_of(u):
        return lax.div(u, chunks)

    def chunk_of(u):
        return lax.rem(u, chunks)

    def strip(ref, u):
        rows = pl.ds(pl.multiple_of(half_of(u) * HALF, HALF), HALF)
        return ref.at[rows, pl.ds(pl.multiple_of(chunk_of(u) * ch, ch), ch)]

    def cot_copy(c):
        return pltpu.make_async_copy(strip(cot, c), cot_v.at[c], local.at[1])

    def hid_copy(c):
        return pltpu.make_async_copy(hid_v.at[c], strip(hidden_out, c), local.at[2])

    own_copies = [pltpu.make_async_copy(inputs.at[:, h], toks.at[h, col], local.at[0]) for h in range(2)]
    for copy in own_copies:
        copy.start()

    @pl.loop(0, chunks)
    def _(c):
        for copy in weight_copies(c):
            copy.start()

    @pl.loop(0, units)
    def _(u):
        cot_copy(u).start()

    barrier = pltpu.get_barrier_semaphore()
    for dev in (left_x, right_x, left_y, right_y, left_z, right_z, far_z, sibling):
        pl.semaphore_signal(barrier, inc=1, device_id=dev, device_id_type=pl.DeviceIdType.MESH)
    def all_landed(ref, sem):
        remote(ref, ref, sem, sem, sibling).wait_recv()

    def all_left(ref, sem):
        remote(ref, ref, sem, sem, sibling).wait_send()

    def mask(c):
        pltpu.make_async_copy(weights.at[c], weights.at[c], ws.at[c]).wait()
        for which, pat in enumerate((gate_pat, up_pat)):
            for i in range(weights.shape[1] // BLOCK):
                for j in range(ch // BLOCK):
                    flag = pat[i, c * (ch // BLOCK) + j].astype(F32)
                    rows, cols = pl.ds(i * BLOCK, BLOCK), pl.ds(which * ch + j * BLOCK, BLOCK)
                    weights[c, rows, cols] = (weights[c, rows, cols].astype(F32) * flag).astype(BF16)

    def mask_some(part_of):
        pl.loop(part_of * chunks // 3, (part_of + 1) * chunks // 3)(mask)

    mask_some(0)
    pl.semaphore_wait(barrier, 8)

    mine, from_m, from_p, from_2 = z * 2 + core, zm * 2 + core, zp * 2 + core, z2 * 2 + core
    both = pl.ds(0, 2)

    def spread(h, src, block, k, dev):
        dst = toks.at[h, block]
        return remote(dst if src is None else src, dst, zsent.at[0], zin.at[h, k], dev)

    def own_sends(h):
        devs = (far_z, left_z, right_z, sibling)
        return [spread(h, inputs.at[:, h], mine, k, dev) for k, dev in enumerate(devs)]

    def shares(h):
        return [spread(h, None, block, 4 + k, sibling) for k, block in enumerate((from_2, from_p, from_m))]

    def gather_start(h):
        sends = own_sends(h)
        for k in (1, 2, 0, 3):
            sends[k].start()

    def gather_share(h):
        for k in (1, 2, 0):
            own_sends(h)[k].wait_recv()
            shares(h)[k].start()

    def gather_end(h):
        own_sends(h)[3].wait_recv()
        for copy in shares(h):
            copy.wait_recv()

    gather_start(0)
    acc[...] = jnp.zeros(acc.shape, F32)
    mask_some(1)
    gather_start(1)
    gather_share(0)
    pltpu.make_async_copy(toks.at[both, 0], toks.at[both, 0], local.at[0]).wait()
    pltpu.make_async_copy(cot_v, cot_v, local.at[1]).wait()
    gather_end(0)

    def copies(c, k):
        a, b = pl.ds(0, ch), pl.ds(ch, ch)
        al, ar, bl, br = pl.ds(0, hc), pl.ds(hc, hc), pl.ds(ch, hc), pl.ds(ch + hc, hc)
        first, second, every = pl.ds(0, 2), pl.ds(2, 2), pl.ds(0, 4)
        rows = pl.ds(0, HALF)
        xdev, ydev = (left_x, right_x), (left_y, right_y)
        if k == 0:
            srcs = (part.at[c, 0, first, x2], part.at[c, 0, second, x2], part.at[c, 1, y2, first], part.at[c, 1, y2, second])
            dsts = tuple(half1.at[c, i // 2, i % 2] for i in range(4))
            devs = xdev + ydev
        elif k == 1:
            srcs = (part.at[c, 0, every, xm], part.at[c, 0, every, xp], part.at[c, 1, ym], part.at[c, 1, yp])
            dsts = tuple(full1.at[c, i // 2, i % 2] for i in range(4))
            devs = xdev + ydev
        elif k == 2:
            srcs = (
                sum1.at[c, 0, y2, rows, al], sum1.at[c, 0, y2, rows, ar],
                sum1.at[c, 1, x2, rows, al], sum1.at[c, 1, x2, rows, ar],
            )
            dsts = tuple(half2.at[c, i // 2, i % 2] for i in range(4))
            devs = ydev + xdev
        elif k == 3:
            srcs = (sum1.at[c, 0, ym], sum1.at[c, 0, yp], sum1.at[c, 1, xm], sum1.at[c, 1, xp])
            dsts = tuple(full2.at[c, i // 2, i % 2] for i in range(4))
            devs = ydev + xdev
        elif k == 4:
            ga, gb = grads.at[c, y, x, rows, a], grads.at[c, y, x, rows, b]
            srcs = dsts = (ga, ga, gb, gb)
            devs = ydev + xdev
        elif k == 5:
            srcs = dsts = (
                grads.at[c, yp, x, rows, ar], grads.at[c, ym, x, rows, al],
                grads.at[c, y, xp, rows, br], grads.at[c, y, xm, rows, bl],
            )
            devs = ydev + xdev
        elif k == 6:
            ga, gb = grads.at[c, every, x, rows, a], grads.at[c, y, every, rows, b]
            srcs = dsts = (ga, ga, gb, gb)
            devs = xdev + ydev
        else:
            srcs = dsts = (
                grads.at[c, second, xp, rows, a], grads.at[c, first, xm, rows, a],
                grads.at[c, yp, second, rows, b], grads.at[c, ym, first, rows, b],
            )
            devs = xdev + ydev
        return [
            remote(s, d, send.at[k], recv.at[chunk_of(c), k], dev)
            for s, d, dev in zip(srcs, dsts, devs)
        ]

    def start(c, k):
        for copy in copies(c, k):
            copy.start()

    sizes = (half1, full1, half2, full2, full2, half2, full1, half1)

    def arrived(c, k):
        all_landed(sizes[k].at[c], recv.at[chunk_of(c), k])

    def f(v):
        return v.astype(F32)

    def forward(c):
        product = jnp.dot(
            toks[half_of(c)].reshape(16 * HALF, toks.shape[4]), weights[chunk_of(c)], preferred_element_type=F32
        ).astype(BF16).reshape(4, 4, HALF, 2 * ch)
        part[c, 0] = product[:, :, :, :ch]
        part[c, 1] = product[:, :, :, ch:]
        start(c, 0)

    def merge1(c):
        arrived(c, 0)
        part[c, 0, 0:2, xm] = (f(part[c, 0, 0:2, xm]) + f(half1[c, 0, 0])).astype(BF16)
        part[c, 0, 2:4, xp] = (f(part[c, 0, 2:4, xp]) + f(half1[c, 0, 1])).astype(BF16)
        part[c, 1, ym, 0:2] = (f(part[c, 1, ym, 0:2]) + f(half1[c, 1, 0])).astype(BF16)
        part[c, 1, yp, 2:4] = (f(part[c, 1, yp, 2:4]) + f(half1[c, 1, 1])).astype(BF16)
        start(c, 1)

    def total1(c):
        arrived(c, 1)
        sum1[c, 0] = (f(part[c, 0, :, x]) + f(full1[c, 0, 0]) + f(full1[c, 0, 1])).astype(BF16)
        sum1[c, 1] = (f(part[c, 1, y]) + f(full1[c, 1, 0]) + f(full1[c, 1, 1])).astype(BF16)
        start(c, 2)

    def merge2(c):
        arrived(c, 2)
        for i, (m, p) in enumerate(((ym, yp), (xm, xp))):
            sum1[c, i, m, :, 0:hc] = (f(sum1[c, i, m, :, 0:hc]) + f(half2[c, i, 0])).astype(BF16)
            sum1[c, i, p, :, hc:ch] = (f(sum1[c, i, p, :, hc:ch]) + f(half2[c, i, 1])).astype(BF16)
        start(c, 3)

    def activate(c):
        arrived(c, 3)
        gate_sum = f(sum1[c, 0, y]) + f(full2[c, 0, 0]) + f(full2[c, 0, 1])
        up_sum = f(sum1[c, 1, x]) + f(full2[c, 1, 0]) + f(full2[c, 1, 1])
        sigmoid_gate = jax.nn.sigmoid(gate_sum)
        activated = gate_sum * sigmoid_gate
        cot_f = f(cot_v[c])
        grads[c, y, x, :, 0:ch] = (
            cot_f * up_sum * sigmoid_gate * (1.0 + gate_sum * (1.0 - sigmoid_gate))
        ).astype(BF16)
        grads[c, y, x, :, ch:2 * ch] = (cot_f * activated).astype(BF16)
        start(c, 4)
        hid_v[c] = (activated * up_sum).astype(BF16)
        hid_copy(c).start()

    def forward1(c):
        arrived(c, 4)
        start(c, 5)

    def spread2(c):
        arrived(c, 5)
        start(c, 6)

    def forward2(c):
        arrived(c, 6)
        start(c, 7)

    width = toks.shape[4] // PIECES

    def back(u, n):
        return lax.dot_general(
            grads[u].reshape(16 * HALF, 2 * ch), weights[chunk_of(u), pl.ds(n * width, width), :],
            (((1,), (1,)), ((), ())), preferred_element_type=F32,
        ).reshape(4, 2, 2, HALF, width)

    def backward(u):
        arrived(u, 7)
        for n in range(PIECES):
            acc[n, half_of(u)] += back(u, n)

    stages = (forward, merge1, total1, merge2, activate, forward1, spread2, forward2, backward)
    final = units - 1

    def z_send(src, dst, k, h, n, dev):
        return remote(src, dst, zsent.at[1], zout.at[k, h, n], dev)

    def z_sib(h, n):
        return z_send(zsend.at[h, n], zsib.at[h, n], 0, h, n, sibling)

    def z_full(h, n):
        pairs = ((z2, far_z), (zm, left_z), (zp, right_z))
        return [z_send(zkeep.at[h, n, to], zfull.at[h, n, k], 1, h, n, dev) for k, (to, dev) in enumerate(pairs)]

    def out_copy(h, n):
        return pltpu.make_async_copy(out_v.at[h, n], grad_out.at[:, h, :, pl.ds(n * width, width)], local.at[3])

    def sum_sibling(h, n):
        zsend[h, n] = acc[n, h, :, other].astype(BF16)
        z_sib(h, n).start()

    def sum_last(h, n):
        acc[n, h] += back(final, n)
        sum_sibling(h, n)

    def sum_cores(h, n):
        all_landed(zsib.at[h, n], zout.at[0, h, n])
        total = acc[n, h, :, core] + f(zsib[h, n])
        acc[n, h, :, core] = total
        zkeep[h, n] = total.astype(BF16)
        for copy in z_full(h, n):
            copy.start()

    def sum_end(h, n):
        all_landed(zfull.at[h, n], zout.at[1, h, n])
        terms = acc[n, h, z, core] + f(zfull[h, n, 0]) + f(zfull[h, n, 1]) + f(zfull[h, n, 2])
        out_v[h, n] = terms.astype(BF16)
        out_copy(h, n).start()

    order = (0, 1, 2, 3, 4, 5, 6, 7, 8)
    steps = units + LAGS[8]

    first_done = chunks + LAGS[8]
    events = [(when, lambda g=g: g(1)) for when, g in zip(GATHER_AT, (gather_share, gather_end))]
    for after, piece in zip(SUM_AFTER, (sum_sibling, sum_cores, sum_end)):
        events.append((first_done + after, lambda p=piece: [p(0, n) for n in range(PIECES)]))

    @pl.loop(0, steps - 1)
    def _(step):
        @pl.when((step >= 2 * chunks // 3) & (step < chunks))
        def _():
            mask(step)

        for when, event in events:

            @pl.when(step == when)
            def _():
                event()

        for k in order:
            u = step - LAGS[k]
            last = final if k == 8 else units

            @pl.when((u >= 0) & (u < last))
            def _():
                stages[k](u)

    arrived(final, 7)
    for piece in (sum_last, sum_cores, sum_end):
        for n in range(PIECES):
            piece(1, n)

    for k in range(8):
        all_left(sizes[k], send.at[k])
    for k in range(2):
        all_left(toks.at[both, pl.ds(0, 7)], zsent.at[k])
    pltpu.make_async_copy(hid_v, hid_v, local.at[2]).wait()
    pltpu.make_async_copy(out_v, out_v, local.at[3]).wait()


def hand_over(hidden, grad, hidden_out, grad_out):
    hidden_out[...] = hidden[...]
    grad_out[...] = grad[...]


def shards(inputs, gate_weight, up_weight, gate_pattern, up_pattern, cotangent):
    tokens, depth = inputs.shape
    hidden = gate_weight.shape[1]
    chunks = hidden // CHUNK
    units = 2 * chunks
    ch = CHUNK
    width = depth // PIECES
    any_spec = pl.BlockSpec(memory_space=pl.ANY)
    smem = pl.BlockSpec(memory_space=pltpu.SMEM)
    dma = pltpu.SemaphoreType.DMA
    scratch = [
        pltpu.VMEM((2, 8, 2, HALF, depth), BF16),
        pltpu.VMEM((chunks, depth, 2 * ch), BF16),
        pltpu.VMEM((units, 2, 4, 4, HALF, ch), BF16),
        pltpu.VMEM((units, 2, 2, 2, HALF, ch), BF16),
        pltpu.VMEM((units, 2, 2, 4, HALF, ch), BF16),
        pltpu.VMEM((units, 2, 4, HALF, ch), BF16),
        pltpu.VMEM((units, 2, 2, HALF, ch // 2), BF16),
        pltpu.VMEM((units, 2, 2, HALF, ch), BF16),
        pltpu.VMEM((units, 4, 4, HALF, 2 * ch), BF16),
        pltpu.VMEM((PIECES, 2, 4, 2, 2, HALF, width), F32),
        pltpu.VMEM((2, PIECES, 4, 2, HALF, width), BF16),
        pltpu.VMEM((2, PIECES, 4, 2, HALF, width), BF16),
        pltpu.VMEM((2, PIECES, 4, 2, HALF, width), BF16),
        pltpu.VMEM((2, PIECES, 3, 2, HALF, width), BF16),
        pltpu.VMEM((units, HALF, ch), BF16),
        pltpu.VMEM((units, HALF, ch), BF16),
        pltpu.VMEM((2, PIECES, 2, HALF, width), BF16),
        dma((8,)),
        dma((chunks, 8)),
        dma((2,)),
        dma((2, 7)),
        dma((2, 2, PIECES)),
        dma((chunks,)),
        dma((4,)),
    ]
    results = pl.pallas_call(
        functools.partial(kernel, chunks),
        out_shape=(
            jax.ShapeDtypeStruct((32, hidden), BF16),
            jax.ShapeDtypeStruct((2, 2, HALF, depth), BF16),
        ),
        in_specs=[any_spec, any_spec, any_spec, smem, smem, any_spec],
        out_specs=(any_spec, any_spec),
        scratch_shapes=scratch,
        compiler_params=pltpu.CompilerParams(
            collective_id=0, has_side_effects=True, vmem_limit_bytes=58 * 1024 * 1024
        ),
        cost_estimate=pl.CostEstimate(
            flops=4 * 512 * depth * 2 * hidden, bytes_accessed=4 * depth * hidden, transcendentals=32 * hidden
        ),
    )(inputs.reshape(2, 2, HALF, depth), gate_weight, up_weight, gate_pattern, up_pattern, cotangent)
    results = (results[0], results[1].reshape(tokens, depth))
    return pl.pallas_call(
        hand_over,
        out_shape=tuple(jax.ShapeDtypeStruct(r.shape, r.dtype) for r in results),
        in_specs=[pl.BlockSpec(memory_space=pltpu.VMEM)] * 2,
        out_specs=(pl.BlockSpec(memory_space=pltpu.VMEM),) * 2,
    )(*results)


def solution(mesh):
    placed = (
        P("col", "row"),
        P("row", "col"),
        P("row", "col"),
        P("row", "col"),
        P("row", "col"),
        P("row", "col"),
    )
    return jax.shard_map(
        shards,
        mesh=mesh,
        in_specs=placed,
        out_specs=(P("row", "col"), P("col", "row")),
        check_vma=False,
    )
```
